128 devices in a mesh: lat: 8 (over y, core), lon: 16 (over z, x).
Axes of the slice: x: 4, y: 4, z: 4, core: 2. Of those that a mesh axis runs over, the one named last changes fastest.
Arguments:
- background: bfloat16 [512, 1024, 128], P('lat', 'lon'), may hold values from -6 to 6
- diffusivity: float32 [512, 1024, 128], P('lat', 'lon'), may hold values from 0.12 to 0.245
- tile_index: int32 [65536, 1], P(('lat', 'lon')), may hold values from 0 to 127; in each aligned block of 512 rows (0 to 511, 512 to 1023, ...) at most 8 rows name the same one
- anchor: int32 [65536], P(('lat', 'lon')), may hold values from 0 to 3968
- weights: float32 [65536, 4], P(('lat', 'lon')), may hold values from 0.2 to 1
- observed: float32 [65536, 128], P(('lat', 'lon')), may hold values from -6 to 6
- accept: int32 [65536, 128], P(('lat', 'lon')), may hold values 0 or 1
- absorb: float32 [128, 128], replicated, may hold values from 0.001 to 0.1
- sensitivity: float32 [128], replicated, may hold values from -0.5 to 0.5
- inverse_variance: float32 [128], replicated, may hold values from 0.25 to 4
Outputs:
- departure: float32 [65536, 128], P(('lat', 'lon'))
- increment: float32 [512, 1024, 128], P('lat', 'lon')
The draws below stay inside these ranges and needn't reach their ends.
Inputs may be any that keep to these rules, and one draw needn't show every extreme that they name: `tile_index`: among the 512 footprints of one device no tile is named more than 8 times, a bound that some block reaches.
All inputs are finite; a program needn't handle non-finite values. No bound on the sum of `accept` on one device may be relied on, other than what follows from the above.
Results may differ from the reference program's by a relative error of at most 0.0003.
Values may be sent and summed in bfloat16 or wider, within the bound.
A program may use at most 64 MiB of HBM per device.

```python
import math
import jax
import jax.numpy as jnp
import numpy as np
from jax import lax

LEV = 128
CHAN = 128
TLAT = 64
TLON = 64
FP_DEV = 512
STEPS = 8
MOST = 8
NLAT = 512
NLON = 1024
FOOT = 65536
N_LON = 16
DEVICES = 128


def draw_background(key, part):
    field = jnp.clip(jax.random.normal(key, (NLAT, NLON, LEV), jnp.float32), -6.0, 6.0)
    return field.astype(jnp.bfloat16)


def draw_diffusivity(key, part):
    uniform_draw = jax.random.uniform(key, (NLAT, NLON, LEV), jnp.float32)
    field = 0.12 + 0.125 * uniform_draw
    return field.astype(jnp.float32)


def plant(values, own_key, least, high):
    dims = values.shape
    index_at = [jax.random.randint(jax.random.fold_in(own_key, axis), (), 0, dims[axis]) for axis in range(len(dims))]
    values = values.at[tuple(index_at)].set(least)
    longest = dims.index(max(dims))
    index_at[longest] = (index_at[longest] + 1) % dims[longest]
    return values.at[tuple(index_at)].set(high)


def level_of(stream_key, shape, shards, smallest, top_value):
    level = 1.0
    for axis_at, parts in shards:
        steps = jax.random.uniform(jax.random.fold_in(jax.random.fold_in(stream_key, 6), axis_at), (parts,), jnp.float32, smallest / len(shards), top_value / len(shards))
        level = level * jnp.repeat(jnp.exp(steps), shape[axis_at] // parts).reshape((-1,) + (1,) * (len(shape) - 1 - axis_at))
    return level


def assign_block(stream_key, own, number, rows, count, top, most, slope):
    sequence = jax.random.permutation(stream_key, count)
    crowded, common = portions_of(count, rows * top, most, slope, True), portions_of(count, rows * top, most, slope, False)
    places = jnp.arange(count)

    def named(tallies, turn):
        used = int((tallies > 0).sum())
        fixed = max(1, used // 4)
        passed = fixed + (places - fixed + turn * (used - fixed)) % max(1, count - fixed)
        return jnp.zeros((count,), jnp.int32).at[sequence[jnp.where(places < fixed, places, passed)]].set(jnp.asarray(tallies, jnp.int32))

    tallies = jnp.where(number % 4 == 0, named(crowded, number // 4), named(common, number - number // 4 - 1))
    mixed = jax.random.permutation(jax.random.fold_in(own, 3), count)
    giver, receiver = mixed[0:count // 2 * 2:2], mixed[1:count // 2 * 2:2]
    room = jnp.minimum(tallies[giver] - 1, most - tallies[receiver]) // 2
    room = jnp.where((giver == sequence[0]) | (receiver == sequence[0]) | (tallies[receiver] == 0), 0, jnp.maximum(room, 0))
    passed = jax.random.randint(jax.random.fold_in(own, 4), (count // 2,), 0, 1 << 20) % (room + 1)
    tallies = tallies.at[giver].add(-passed).at[receiver].add(passed)
    members = jnp.searchsorted(jnp.cumsum(tallies), jnp.arange(rows * top), side="right").astype(jnp.int32)
    grid = members.reshape(top, rows).T
    grid = grid[jax.random.permutation(jax.random.fold_in(own, 1), rows)]
    turn = jax.random.randint(jax.random.fold_in(own, 2), (rows, 1), 0, top)
    return jnp.take_along_axis(grid, (jnp.arange(top)[None, :] + turn) % top, axis=1)


def portions_of(number_of, total, most, lean, full):
    weights = [(1 << 20) // math.isqrt(rank ** lean) + 1 for rank in range(1, number_of + 1)]
    largest = most if full else min(most, max(-(-total // number_of), total * weights[0] // sum(weights)))
    least = 1 if total - largest >= number_of - 1 else 0
    given, rest = [largest] + [least] * (number_of - 1), total - largest - least * (number_of - 1)
    while rest > 0:
        candidates = [i for i in range(1, number_of) if given[i] < largest] or [i for i in range(1, number_of) if given[i] < most]
        whole, left = sum([weights[i] for i in candidates]), rest
        for i in candidates:
            extra = min(most - given[i], max(1, left * weights[i] // whole), rest)
            given[i] = given[i] + extra
            rest = rest - extra
    return np.array(given)


def bell_draw(stream_key, dims, width, bound, shards=(), held_as=jnp.bfloat16):
    array = width * jax.random.normal(stream_key, dims, jnp.float32)
    if shards:
        array = array * level_of(stream_key, dims, shards, -0.22, 0.18)
    return jnp.clip(array, -bound, bound).astype(held_as)


def setup_inputs(seed: int = 0) -> dict:
    seeds = jax.random.split(jax.random.key(seed), 11)
    background = draw_background(jax.random.fold_in(seeds[10], 71), 0)
    diffusivity = draw_diffusivity(jax.random.fold_in(seeds[10], 71), 0)
    tile_index_keys = jax.random.split(jax.random.fold_in(seeds[2], 1), FOOT // FP_DEV)
    tile_index_turns = jax.random.permutation(jax.random.fold_in(seeds[2], 3), FOOT // FP_DEV)
    tile_index = jax.vmap(lambda own, number: assign_block(jax.random.fold_in(seeds[2], 2), own, number, FP_DEV, DEVICES, 1, MOST, 1))(tile_index_keys, tile_index_turns).reshape((FOOT, 1))
    anchor = plant(jax.random.randint(seeds[3], (FOOT,), 0, (TLAT - 1) * (TLON - 1)), jax.random.fold_in(seeds[3], 1), 0, ((TLAT - 1) * (TLON - 1)) - 1).astype(jnp.int32)
    weights = jnp.clip(jnp.exp(math.log(1.0) - 1.609438 * jax.random.uniform(seeds[4], (FOOT, 4), jnp.float32) ** level_of(seeds[4], (FOOT, 4), ((0, 128),), -0.2, 0.2)), 0.2, 1.0)
    observed = bell_draw(seeds[5], (FOOT, CHAN), 1.0, 6.0, ((0, 128),), jnp.float32)
    accept = plant((jax.random.randint(seeds[6], (FOOT, CHAN), 0, 4) < 3).astype(jnp.int32), jax.random.fold_in(seeds[6], 1), 0, 1)
    absorb = jnp.clip(jnp.exp(jax.random.uniform(seeds[7], (LEV, CHAN), jnp.float32, math.log(0.001), math.log(0.1))), 0.001, 0.1)
    sensitivity = jnp.clip(jax.random.uniform(seeds[8], (CHAN,), jnp.float32, -0.5, 0.5), -0.5, 0.5)
    inverse_variance = jnp.clip(jnp.exp(jax.random.uniform(seeds[9], (CHAN,), jnp.float32, math.log(0.25), math.log(4.0))), 0.25, 4.0)
    return dict(background=background, diffusivity=diffusivity, tile_index=tile_index, anchor=anchor, weights=weights, observed=observed, accept=accept, absorb=absorb, sensitivity=sensitivity, inverse_variance=inverse_variance)


NEIGHBOURS = ((-1, 0), (1, 0), (0, -1), (0, 1))

def evolve(profile, absorb, sensitivity):
    layer_depth = absorb[None, :, :] * jnp.exp(sensitivity[None, None, :] * profile[:, :, None])
    optical = jnp.cumsum(layer_depth, axis=1)
    transmit = jnp.exp(-optical)
    transmit_above = jnp.concatenate([jnp.ones_like(transmit[:, :1, :]), transmit[:, :-1, :]], axis=1)
    layered = lax.optimization_barrier(jnp.sum(profile[:, :, None] * (transmit_above - transmit), axis=1))
    return layered + profile[:, -1:] * transmit[:, -1, :]

def assess(profile, observed, accept, absorb, sensitivity, inverse_variance):
    evolved, pullback = jax.vjp(lambda prof_in: evolve(prof_in, absorb, sensitivity), profile)
    departure = observed - evolved
    adjoint, = pullback(-(accept.astype(jnp.float32) * inverse_variance[None, :] * departure))
    return (departure, adjoint)

def shift_rows(grid_field, offset):
    zero_row = jnp.zeros_like(grid_field[:1])
    if offset < 0:
        return jnp.concatenate([zero_row, grid_field[:-1]], axis=0)
    return jnp.concatenate([grid_field[1:], zero_row], axis=0)

def relax_global(grid_field, diffusivity):
    summed = grid_field
    for d_row, d_col in NEIGHBOURS:
        if d_row != 0:
            neighbour = shift_rows(grid_field, d_row)
            kappa_near = shift_rows(diffusivity, d_row)
        else:
            neighbour = jnp.roll(grid_field, -d_col, axis=1)
            kappa_near = jnp.roll(diffusivity, -d_col, axis=1)
        summed = summed + 0.5 * (diffusivity + kappa_near) * (neighbour - grid_field)
    return summed

def reference(background, diffusivity, tile_index, anchor, weights, observed, accept, absorb, sensitivity, inverse_variance):
    owner_tile = tile_index[:, 0]
    base_row = owner_tile // N_LON * TLAT + anchor // (TLON - 1)
    base_col = owner_tile % N_LON * TLON + anchor % (TLON - 1)
    row_ids = jnp.stack([base_row, base_row, base_row + 1, base_row + 1], axis=1)
    col_ids = jnp.stack([base_col, base_col + 1, base_col, base_col + 1], axis=1)
    column_ids = (row_ids * NLON + col_ids).astype(jnp.int32)
    shares = weights / lax.optimization_barrier(jnp.sum(weights, axis=1, keepdims=True))
    flat_bg = background.reshape(NLAT * NLON, LEV)
    profile = lax.optimization_barrier(jnp.sum(shares[:, :, None] * flat_bg[column_ids].astype(jnp.float32), axis=1))
    block_count = FOOT // 1024
    departure, adjoint = lax.map(lambda packed: assess(packed[0], packed[1], packed[2], absorb, sensitivity, inverse_variance), (profile.reshape(block_count, 1024, LEV), observed.reshape(block_count, 1024, CHAN), accept.reshape(block_count, 1024, CHAN)))
    departure = departure.reshape(FOOT, CHAN)
    adjoint = adjoint.reshape(FOOT, LEV)
    adjoint_terms = -(shares[:, :, None] * adjoint[:, None, :])
    increment = jnp.zeros((NLAT * NLON, LEV), jnp.float32).at[column_ids.reshape(-1)].add(adjoint_terms.reshape(FOOT * 4, LEV))
    grid_field = increment.reshape(NLAT, NLON, LEV)
    for repeat_index in range(STEPS):
        grid_field = relax_global(grid_field, diffusivity)
    return (departure, grid_field)
```

```python
import functools

import jax
import jax.numpy as jnp
from jax import lax
from jax.experimental import pallas as pl
from jax.experimental.pallas import tpu as pltpu
from jax.sharding import PartitionSpec as P

STEPS = 8
HALO = 8
SUB = 8
LANES = 128
LOG2E = 1.4426950408889634
LN2 = 0.6931471805599453
FIXED = 2.0**30
F32 = jnp.float32
BF16 = jnp.bfloat16
I32 = jnp.int32
MESH = pl.DeviceIdType.MESH
VMEM_SPEC = pl.BlockSpec(memory_space=pltpu.VMEM)
SMEM_SPEC = pl.BlockSpec(memory_space=pltpu.SMEM)
ANY_SPEC = pl.BlockSpec(memory_space=pl.ANY)
VMEM_BYTES = 56 * 2**20


def pieces(x):
    high = x.astype(BF16)
    rest = x - high.astype(F32)
    middle = rest.astype(BF16)
    low = (rest - middle.astype(F32)).astype(BF16)
    return high, middle, low


def dot(a, b, contract):
    return lax.dot_general(a, b, (contract, ((), ())), preferred_element_type=F32)


def request_kernel(cap, tile_ref, anchor_ref, weights_ref, slot_ref, request_ref):
    dev_count, _, width = request_ref.shape
    feet = tile_ref.shape[1]
    tile = tile_ref[...]
    named = lax.broadcasted_iota(I32, (dev_count, feet), 0) == tile
    onehot = named.astype(F32).astype(BF16)
    before = (
        lax.broadcasted_iota(I32, (feet, feet), 0) < lax.broadcasted_iota(I32, (feet, feet), 1)
    )
    earlier = dot(onehot, before.astype(F32).astype(BF16), ((1,), (0,)))
    rank = jnp.sum(jnp.where(named, earlier, 0.0), axis=0, keepdims=True).astype(I32)
    slot_ref[...] = tile * cap + rank
    anchor = anchor_ref[...]
    row = ((anchor.astype(F32) + 0.5) * (1.0 / 63.0)).astype(I32)
    base = (anchor + row).astype(F32)
    weights = weights_ref[...]
    shares = weights / jnp.sum(weights, axis=0, keepdims=True)
    place = lax.broadcasted_iota(I32, (cap, feet), 0) == rank
    fields = [base] + [shares[k : k + 1, :] for k in range(4)]
    rows = [jnp.where(place, field, 0.0) for field in fields]
    if width > 5 * cap:
        rows.append(jnp.zeros((width - 5 * cap, feet), F32))
    packed = jnp.concatenate(rows, axis=0)
    high, middle, low = pieces(packed)
    last = ((1,), (1,))
    message = dot(onehot, high, last) + dot(onehot, middle, last) + dot(onehot, low, last)
    scaled = jnp.where(
        lax.broadcasted_iota(I32, (dev_count, width), 1) < cap, message, message * FIXED
    )
    request_ref[...] = scaled.astype(I32).reshape(dev_count, 1, width)


def coordinates(index, lon_count):
    return (index // lon_count, lax.rem(index, lon_count))


def my_index(lon_count):
    return lax.axis_index("lat") * lon_count + lax.axis_index("lon")


def greet_all(me, dev_count, lon_count):
    barrier = pltpu.get_barrier_semaphore()

    @pl.loop(1, dev_count)
    def _(d):
        other = lax.rem(me + d, dev_count)
        pl.semaphore_signal(
            barrier, inc=1, device_id=coordinates(other, lon_count), device_id_type=MESH
        )

    return barrier


def columns_kernel(
    cap,
    lon_count,
    request_ref,
    background_ref,
    asked_ref,
    profile_ref,
    field,
    found,
    asked_smem,
    ask_send,
    ask_recv,
    back_send,
    back_recv,
    local_sem,
):
    dev_count = request_ref.shape[0]
    me = my_index(lon_count)
    tile_cols = 64
    barrier = greet_all(me, dev_count, lon_count)

    chunk = 256

    @pl.loop(0, background_ref.shape[0] // chunk)
    def _(j):
        at = pl.ds(pl.multiple_of(j * chunk, chunk), chunk)
        field[at, :] = background_ref[at, :].astype(F32)

    pl.semaphore_wait(barrier, dev_count - 1)

    def ask(other):
        return pltpu.make_async_remote_copy(
            src_ref=request_ref.at[other],
            dst_ref=asked_ref.at[me],
            send_sem=ask_send.at[other],
            recv_sem=ask_recv.at[me],
            device_id=coordinates(other, lon_count),
            device_id_type=MESH,
        )

    def ask_from(other):
        return pltpu.make_async_remote_copy(
            src_ref=request_ref.at[other],
            dst_ref=asked_ref.at[other],
            send_sem=ask_send.at[other],
            recv_sem=ask_recv.at[other],
            device_id=coordinates(other, lon_count),
            device_id_type=MESH,
        )

    @pl.loop(1, dev_count)
    def _(d):
        ask(lax.rem(me + d, dev_count)).start()

    asked_ref[me] = request_ref[me]

    @pl.loop(1, dev_count)
    def _(d):
        ask_from(lax.rem(me + d, dev_count)).wait_recv()

    to_smem = pltpu.make_async_copy(asked_ref, asked_smem, local_sem)
    to_smem.start()
    to_smem.wait()

    def gather(source):
        for r in range(cap):
            at = asked_smem[source, 0, r]
            total = None
            for k, offset in enumerate((0, 1, tile_cols, tile_cols + 1)):
                share = asked_smem[source, 0, (k + 1) * cap + r].astype(F32)
                term = share * field[pl.ds(at + offset, 1), :]
                total = term if total is None else total + term
            found[source, r : r + 1, :] = total * (1.0 / FIXED)

    def back(source):
        return pltpu.make_async_remote_copy(
            src_ref=found.at[source],
            dst_ref=profile_ref.at[me],
            send_sem=back_send.at[source],
            recv_sem=back_recv.at[me],
            device_id=coordinates(source, lon_count),
            device_id_type=MESH,
        )

    def back_from(other):
        return pltpu.make_async_remote_copy(
            src_ref=found.at[other],
            dst_ref=profile_ref.at[other],
            send_sem=back_send.at[other],
            recv_sem=back_recv.at[other],
            device_id=coordinates(other, lon_count),
            device_id_type=MESH,
        )

    @pl.loop(1, dev_count)
    def _(d):
        source = lax.rem(me + d, dev_count)
        gather(source)
        back(source).start()

    gather(me)
    profile_ref[me] = found[me]

    @pl.loop(1, dev_count)
    def _(d):
        other = lax.rem(me + d, dev_count)
        ask(other).wait_send()
        back(other).wait_send()
        back_from(other).wait_recv()


def exchange_kernel(lon_count, given_ref, taken_ref, send, recv):
    dev_count = given_ref.shape[0]
    me = my_index(lon_count)
    barrier = greet_all(me, dev_count, lon_count)
    taken_ref[me] = given_ref[me]
    pl.semaphore_wait(barrier, dev_count - 1)

    def give(other):
        return pltpu.make_async_remote_copy(
            src_ref=given_ref.at[other],
            dst_ref=taken_ref.at[me],
            send_sem=send.at[other],
            recv_sem=recv.at[me],
            device_id=coordinates(other, lon_count),
            device_id_type=MESH,
        )

    def take(other):
        return pltpu.make_async_remote_copy(
            src_ref=given_ref.at[other],
            dst_ref=taken_ref.at[other],
            send_sem=send.at[other],
            recv_sem=recv.at[other],
            device_id=coordinates(other, lon_count),
            device_id_type=MESH,
        )

    @pl.loop(1, dev_count)
    def _(d):
        give(lax.rem(me + d, dev_count)).start()

    @pl.loop(1, dev_count)
    def _(d):
        other = lax.rem(me + d, dev_count)
        give(other).wait_send()
        take(other).wait_recv()


def assess_kernel(
    slot_ref,
    arrived_ref,
    observed_ref,
    accept_ref,
    absorb_ref,
    sensitivity_ref,
    variance_ref,
    departure_ref,
    grad_ref,
    chosen,
    profile,
    slope,
    weight,
    absorb_wide,
    sens_log,
    sens_ln,
    depth,
    transmit,
    sums,
    adjoint,
):
    slots, levels = arrived_ref.shape
    feet, channels = observed_ref.shape
    groups = feet // LANES
    parts = channels // SUB

    wide = lambda row: jnp.swapaxes(jnp.broadcast_to(row, (LANES, channels)), 0, 1)
    sens = wide(sensitivity_ref[...])
    sens_log[...] = sens * LOG2E
    sens_ln[...] = sens * LN2

    absorb_t = jnp.swapaxes(absorb_ref[...] * (-LOG2E), 0, 1)

    @pl.loop(0, levels // SUB)
    def _(j):
        turned = pltpu.roll(absorb_t, lax.rem(levels - j * SUB, levels), 1)
        for i in range(SUB):
            absorb_wide[j * SUB + i] = jnp.broadcast_to(turned[:, i : i + 1], (channels, LANES))

    block = 256 if slots % 256 == 0 else slots

    @pl.loop(0, slots // block)
    def _(j):
        first = pl.multiple_of(j * block, block)
        here = lax.broadcasted_iota(I32, (block, feet), 0) + first == slot_ref[...]
        chosen[pl.ds(first, block), :] = here.astype(F32).astype(BF16)

    arrived_t = jnp.swapaxes(arrived_ref[...], 0, 1)
    high, middle, low = pieces(arrived_t)
    plain = ((1,), (0,))
    mine = dot(high, chosen[...], plain) + dot(middle, chosen[...], plain) + dot(low, chosen[...], plain)
    below = jnp.concatenate([mine[1:, :], mine[levels - 1 :, :]], axis=0)
    for g in range(groups):
        at = slice(g * LANES, (g + 1) * LANES)
        profile[g] = mine[:, at]
        slope[g] = below[:, at] - mine[:, at]

    for g in range(groups):
        at = pl.ds(g * LANES, LANES)
        accepted = accept_ref[at, :].astype(F32) * variance_ref[...]
        weight[:, at] = jnp.swapaxes(accepted, 0, 1)

    level = lax.broadcasted_iota(I32, (levels, levels * SUB), 0)
    source = lax.broadcasted_iota(I32, (levels, levels * SUB), 1) // SUB
    same = (level == source).astype(F32)
    fall = (level == source + 1).astype(F32) - jnp.where(level == levels - 1, 0.0, same)
    same = same.astype(BF16)
    fall = fall.astype(BF16)

    for g in range(groups):
        at = pl.ds(g * LANES, LANES)

        def descend(l, carry):
            p = profile[g, pl.ds(l, 1), :]
            q = slope[g, pl.ds(l, 1), :]
            out = []
            for c in range(parts):
                rows = slice(c * SUB, (c + 1) * SUB)
                optical, evolved = carry[c]
                layer = absorb_wide[l, rows, :] * jnp.exp2(sens_log[rows, :] * p)
                optical = optical + layer
                passed = jnp.exp2(optical)
                depth[l, rows, :] = layer
                transmit[l, rows, :] = passed
                out.append((optical, evolved + q * passed))
            return tuple(out)

        zero = jnp.zeros((SUB, LANES), F32)
        done = lax.fori_loop(0, levels, descend, ((zero, zero),) * parts, unroll=2)
        top = profile[g, 0:1, :]
        observed_t = jnp.swapaxes(observed_ref[at, :], 0, 1)
        departed = []
        pulls = []
        for c in range(parts):
            rows = slice(c * SUB, (c + 1) * SUB)
            part = observed_t[rows, :] - (done[c][1] + top)
            departed.append(part)
            pulls.append(-(weight[rows, at] * part))
        departure_ref[at, :] = jnp.swapaxes(jnp.concatenate(departed, axis=0), 0, 1)
        whole = pulls[0]
        for c in range(1, parts):
            whole = whole + pulls[c]
        whole = jnp.sum(whole, axis=0, keepdims=True)
        transmit_pull = tuple(pulls)

        def ascend(step, carry):
            l = levels - 1 - step
            q = slope[g, pl.ds(l, 1), :]
            out = []
            passed_sum = None
            layer_sum = None
            for c in range(parts):
                rows = slice(c * SUB, (c + 1) * SUB)
                pulled = transmit_pull[c] * transmit[l, rows, :]
                rest = carry[c] + q * pulled
                through = sens_ln[rows, :] * (depth[l, rows, :] * rest)
                passed_sum = pulled if c == 0 else passed_sum + pulled
                layer_sum = through if c == 0 else layer_sum + through
                out.append(rest)
            at_l = pl.ds(pl.multiple_of(l * SUB, SUB), SUB)
            sums[0, at_l, :] = passed_sum
            sums[1, at_l, :] = layer_sum
            return tuple(out)

        lax.fori_loop(0, levels, ascend, (zero,) * parts, unroll=2)
        total = None
        for matrix, index in ((fall, 0), (same, 1)):
            for piece in pieces(sums[index]):
                term = dot(matrix, piece, plain)
                total = term if total is None else total + term
        first = lax.broadcasted_iota(I32, (levels, LANES), 0) == 0
        adjoint[:, at] = total + jnp.where(first, whole, 0.0)

    parts_adjoint = pieces(adjoint[...])

    @pl.loop(0, slots // block)
    def _(j):
        rows = pl.ds(pl.multiple_of(j * block, block), block)
        total = None
        for piece in parts_adjoint:
            term = dot(chosen[rows, :], piece, ((1,), (1,)))
            total = term if total is None else total + term
        grad_ref[rows, :] = total


def spread_kernel(cap, asked_ref, arrived_ref, raw_ref, other):
    tile_cols = 64
    cells, levels = raw_ref.shape
    chunk = 256

    @pl.loop(0, cells // chunk)
    def _(j):
        at = pl.ds(pl.multiple_of(j * chunk, chunk), chunk)
        raw_ref[at, :] = jnp.zeros((chunk, levels), F32)
        other[at, :] = jnp.zeros((chunk, levels), F32)

    @pl.loop(0, asked_ref.shape[0])
    def _(source):
        for r in range(0, cap, 2):
            for total, row in ((raw_ref, r), (other, r + 1)):
                at = asked_ref[source, 0, row]
                value = arrived_ref[source, row : row + 1, :]
                sites = [pl.ds(at + o, 1) for o in (0, 1, tile_cols, tile_cols + 1)]
                fresh = []
                for k in range(4):
                    share = asked_ref[source, 0, (k + 1) * cap + row].astype(F32)
                    fresh.append(total[sites[k], :] + share * value)
                for k in range(4):
                    total[sites[k], :] = fresh[k]

    @pl.loop(0, cells // chunk)
    def _(j):
        at = pl.ds(pl.multiple_of(j * chunk, chunk), chunk)
        raw_ref[at, :] = (raw_ref[at, :] + other[at, :]) * (-1.0 / FIXED)


def diffuse_kernel(
    lat_count,
    lon_count,
    raw_ref,
    kappa_ref,
    out_ref,
    field_in,
    kappa_in,
    field,
    east,
    south,
    local_sems,
    send_sems,
    recv_sems,
):
    height, breadth, levels = raw_ref.shape
    tall = height + 2 * HALO
    count = (breadth + 2 * HALO) // SUB
    lat = lax.axis_index("lat")
    lon = lax.axis_index("lon")
    is_first = lat == 0
    is_last = lat == lat_count - 1

    directions = [(a, b) for a in (-1, 0, 1) for b in (-1, 0, 1) if (a, b) != (0, 0)]

    def there(a):
        return jnp.logical_and(lat + a >= 0, lat + a < lat_count)

    def device(a, b):
        return (lat + a, lax.rem(lon + b + lon_count, lon_count))

    barrier = pltpu.get_barrier_semaphore()
    for a, b in directions:

        @pl.when(there(a))
        def _(a=a, b=b):
            pl.semaphore_signal(barrier, inc=1, device_id=device(a, b), device_id_type=MESH)

    own = []
    centre = (pl.ds(HALO, height), pl.ds(HALO, breadth))
    for n, (source, target) in enumerate(((kappa_ref, kappa_in), (raw_ref, field_in))):
        copy = pltpu.make_async_copy(source, target.at[centre], local_sems.at[n])
        copy.start()
        own.append(copy)

    zero_rows = jnp.zeros((HALO, breadth + 2 * HALO, levels), F32)
    flat_rows = jnp.zeros((HALO, count, SUB, levels), F32)

    @pl.when(is_first)
    def _():
        kappa_in[pl.ds(0, HALO)] = zero_rows
        field_in[pl.ds(0, HALO)] = zero_rows
        field[pl.ds(0, HALO)] = flat_rows

    @pl.when(is_last)
    def _():
        kappa_in[pl.ds(HALO + height, HALO)] = zero_rows
        field_in[pl.ds(HALO + height, HALO)] = zero_rows
        field[pl.ds(HALO + height, HALO)] = flat_rows

    neighbours = 8 - 3 * is_first.astype(I32) - 3 * is_last.astype(I32)
    pl.semaphore_wait(barrier, neighbours)

    def span(step, size):
        given = {-1: pl.ds(0, HALO), 0: pl.ds(0, size), 1: pl.ds(size - HALO, HALO)}[step]
        taken = {-1: pl.ds(HALO + size, HALO), 0: pl.ds(HALO, size), 1: pl.ds(0, HALO)}[step]
        return given, taken

    def edge(array, n):
        a, b = directions[n]
        source, target = ((kappa_ref, kappa_in), (raw_ref, field_in))[array]
        given_rows, taken_rows = span(a, height)
        given_cols, taken_cols = span(b, breadth)
        return pltpu.make_async_remote_copy(
            src_ref=source.at[given_rows, given_cols],
            dst_ref=target.at[taken_rows, taken_cols],
            send_sem=send_sems.at[array, n],
            recv_sem=recv_sems.at[array, n],
            device_id=device(a, b),
            device_id_type=MESH,
        )

    for array in range(2):
        for n, (a, b) in enumerate(directions):

            @pl.when(there(a))
            def _(array=array, n=n):
                edge(array, n).start()

    def arrive(array):
        own[array].wait()
        for n, (a, b) in enumerate(directions):

            @pl.when(there(-a))
            def _(n=n):
                edge(array, n).wait_recv()

    def strided(ref, r):
        return tuple(ref[r, pl.ds(i, SUB, stride=count), :] for i in range(count))

    def later(x):
        return pltpu.roll(x, SUB - 1, 0)

    def sooner(x):
        return pltpu.roll(x, 1, 0)

    arrive(0)

    def conduct(r, here):
        below = strided(kappa_in, jnp.minimum(r + 1, tall - 1))
        for i in range(count):
            beside = here[i + 1] if i + 1 < count else later(here[0])
            east[r, i] = 0.5 * (here[i] + beside)
            south[r, i] = 0.5 * (here[i] + below[i])
        return below

    lax.fori_loop(0, tall, conduct, strided(kappa_in, 0))
    arrive(1)

    def plain(ref, r):
        return tuple(ref[r, i] for i in range(count))

    for step in range(1, STEPS + 1):
        low = jnp.where(is_first, HALO, step)
        high = jnp.where(is_last, HALO + height, tall - step)
        if step == 1:
            load = functools.partial(strided, field_in)
        else:
            load = functools.partial(plain, field)

        def relax(r, carry, load=load, step=step):
            here, above = carry
            below = load(r + 1)
            down = [south[r, i] * (below[i] - here[i]) for i in range(count)]
            right = []
            for i in range(count):
                beside = here[i + 1] if i + 1 < count else later(here[0])
                right.append(east[r, i] * (beside - here[i]))
            for i in range(count):
                left = right[i - 1] if i > 0 else sooner(right[count - 1])
                new = here[i] + ((right[i] - left) + (down[i] - above[i]))
                if step == STEPS:
                    field_in[r, pl.ds(i, SUB, stride=count), :] = new
                else:
                    field[r, i] = new
            return below, tuple(down)

        before = load(low - 1)
        here = load(low)
        above = tuple(south[low - 1, i] * (here[i] - before[i]) for i in range(count))
        lax.fori_loop(low, high, relax, (here, above))

    result = pltpu.make_async_copy(field_in.at[centre], out_ref, local_sems.at[0])
    result.start()
    for array in range(2):
        for n, (a, b) in enumerate(directions):

            @pl.when(there(a))
            def _(array=array, n=n):
                edge(array, n).wait_send()

    result.wait()


def local(
    lat_count,
    lon_count,
    background,
    diffusivity,
    tile_index,
    anchor,
    weights,
    observed,
    accept,
    absorb,
    sensitivity,
    inverse_variance,
):
    dev_count = lat_count * lon_count
    feet, channels = observed.shape
    cap = max(2, 2 * feet // dev_count)
    height, breadth, levels = background.shape
    slots = dev_count * cap
    width = -(-5 * cap // LANES) * LANES
    shape = jax.ShapeDtypeStruct
    params = functools.partial(pltpu.CompilerParams, vmem_limit_bytes=VMEM_BYTES)
    dma = pltpu.SemaphoreType.DMA

    slot, request = pl.pallas_call(
        functools.partial(request_kernel, cap),
        out_shape=(shape((1, feet), I32), shape((dev_count, 1, width), I32)),
        in_specs=[VMEM_SPEC] * 3,
        out_specs=(VMEM_SPEC, VMEM_SPEC),
        compiler_params=params(),
        name="request",
    )(tile_index.reshape(1, feet), anchor.reshape(1, feet), weights.T)

    asked, arrived = pl.pallas_call(
        functools.partial(columns_kernel, cap, lon_count),
        out_shape=(
            shape((dev_count, 1, width), I32),
            shape((dev_count, cap, levels), F32),
        ),
        in_specs=[VMEM_SPEC] * 2,
        out_specs=(VMEM_SPEC, VMEM_SPEC),
        scratch_shapes=[
            pltpu.VMEM((height * breadth, levels), F32),
            pltpu.VMEM((dev_count, cap, levels), F32),
            pltpu.SMEM((dev_count, 1, width), I32),
            dma((dev_count,)),
            dma((dev_count,)),
            dma((dev_count,)),
            dma((dev_count,)),
            dma,
        ],
        compiler_params=params(collective_id=0, has_side_effects=True),
        name="columns",
    )(request, background.reshape(height * breadth, levels))

    departure, grad = pl.pallas_call(
        assess_kernel,
        out_shape=(shape((feet, channels), F32), shape((slots, levels), F32)),
        in_specs=[VMEM_SPEC] * 7,
        out_specs=(VMEM_SPEC, VMEM_SPEC),
        scratch_shapes=[
            pltpu.VMEM((slots, feet), BF16),
            pltpu.VMEM((feet // LANES, levels, LANES), F32),
            pltpu.VMEM((feet // LANES, levels, LANES), F32),
            pltpu.VMEM((channels, feet), F32),
            pltpu.VMEM((levels, channels, LANES), F32),
            pltpu.VMEM((channels, LANES), F32),
            pltpu.VMEM((channels, LANES), F32),
            pltpu.VMEM((levels, channels, LANES), F32),
            pltpu.VMEM((levels, channels, LANES), F32),
            pltpu.VMEM((2, levels * SUB, LANES), F32),
            pltpu.VMEM((levels, feet), F32),
        ],
        compiler_params=params(),
        name="assess",
    )(
        slot,
        arrived.reshape(slots, levels),
        observed,
        accept,
        absorb,
        sensitivity.reshape(1, channels),
        inverse_variance.reshape(1, channels),
    )

    pulled = pl.pallas_call(
        functools.partial(exchange_kernel, lon_count),
        out_shape=shape((dev_count, cap, levels), F32),
        in_specs=[VMEM_SPEC],
        out_specs=VMEM_SPEC,
        scratch_shapes=[dma((dev_count,)), dma((dev_count,))],
        compiler_params=params(collective_id=1, has_side_effects=True),
        name="exchange",
    )(grad.reshape(dev_count, cap, levels))

    raw = pl.pallas_call(
        functools.partial(spread_kernel, cap),
        out_shape=shape((height * breadth, levels), F32),
        in_specs=[SMEM_SPEC, VMEM_SPEC],
        out_specs=VMEM_SPEC,
        scratch_shapes=[pltpu.VMEM((height * breadth, levels), F32)],
        compiler_params=params(),
        name="spread",
    )(asked, pulled)

    wide = (height + 2 * HALO, breadth + 2 * HALO, levels)
    turned = (height + 2 * HALO, (breadth + 2 * HALO) // SUB, SUB, levels)
    increment = pl.pallas_call(
        functools.partial(diffuse_kernel, lat_count, lon_count),
        out_shape=shape((height, breadth, levels), F32),
        in_specs=[ANY_SPEC, ANY_SPEC],
        out_specs=ANY_SPEC,
        scratch_shapes=[
            pltpu.VMEM(wide, F32),
            pltpu.VMEM(wide, F32),
            pltpu.VMEM(turned, F32),
            pltpu.VMEM(turned, F32),
            pltpu.VMEM(turned, F32),
            dma((2,)),
            dma((2, 8)),
            dma((2, 8)),
        ],
        compiler_params=params(collective_id=2, has_side_effects=True),
        name="diffuse",
    )(raw.reshape(height, breadth, levels), diffusivity)
    return (departure, increment)


def solution(mesh):
    in_specs = (
        P("lat", "lon", None),
        P("lat", "lon", None),
        P(("lat", "lon"), None),
        P(("lat", "lon")),
        P(("lat", "lon"), None),
        P(("lat", "lon"), None),
        P(("lat", "lon"), None),
        P(),
        P(),
        P(),
    )
    out_specs = (P(("lat", "lon"), None), P("lat", "lon", None))
    return jax.shard_map(
        functools.partial(local, mesh.shape["lat"], mesh.shape["lon"]),
        mesh=mesh,
        in_specs=in_specs,
        out_specs=out_specs,
        check_vma=False,
    )
```

```python
import functools

import jax
import jax.numpy as jnp
from jax import lax
from jax.experimental import pallas as pl
from jax.experimental.pallas import tpu as pltpu
from jax.sharding import PartitionSpec as P

STEPS = 8
HALO = 8
SUB = 8
LANES = 128
LOG2E = 1.4426950408889634
LN2 = 0.6931471805599453
FIXED = 2.0**30
F32 = jnp.float32
BF16 = jnp.bfloat16
I32 = jnp.int32
MESH = pl.DeviceIdType.MESH
VMEM_SPEC = pl.BlockSpec(memory_space=pltpu.VMEM)
SMEM_SPEC = pl.BlockSpec(memory_space=pltpu.SMEM)
ANY_SPEC = pl.BlockSpec(memory_space=pl.ANY)
VMEM_BYTES = 56 * 2**20


def pieces(x):
    high = x.astype(BF16)
    rest = x - high.astype(F32)
    middle = rest.astype(BF16)
    low = (rest - middle.astype(F32)).astype(BF16)
    return high, middle, low


def dot(a, b, contract):
    return lax.dot_general(a, b, (contract, ((), ())), preferred_element_type=F32)


def request_kernel(cap, tile_ref, anchor_ref, weights_ref, slot_ref, request_ref):
    dev_count, _, width = request_ref.shape
    feet = tile_ref.shape[1]
    tile = tile_ref[...]
    named = lax.broadcasted_iota(I32, (dev_count, feet), 0) == tile
    onehot = named.astype(F32).astype(BF16)
    before = (
        lax.broadcasted_iota(I32, (feet, feet), 0) < lax.broadcasted_iota(I32, (feet, feet), 1)
    )
    earlier = dot(onehot, before.astype(F32).astype(BF16), ((1,), (0,)))
    rank = jnp.sum(jnp.where(named, earlier, 0.0), axis=0, keepdims=True).astype(I32)
    slot_ref[...] = tile * cap + rank
    anchor = anchor_ref[...]
    row = ((anchor.astype(F32) + 0.5) * (1.0 / 63.0)).astype(I32)
    base = (anchor + row).astype(F32)
    weights = weights_ref[...]
    shares = weights / jnp.sum(weights, axis=0, keepdims=True)
    place = lax.broadcasted_iota(I32, (cap, feet), 0) == rank
    fields = [base] + [shares[k : k + 1, :] for k in range(4)]
    rows = [jnp.where(place, field, 0.0) for field in fields]
    if width > 5 * cap:
        rows.append(jnp.zeros((width - 5 * cap, feet), F32))
    packed = jnp.concatenate(rows, axis=0)
    high, middle, low = pieces(packed)
    last = ((1,), (1,))
    message = dot(onehot, high, last) + dot(onehot, middle, last) + dot(onehot, low, last)
    scaled = jnp.where(
        lax.broadcasted_iota(I32, (dev_count, width), 1) < cap, message, message * FIXED
    )
    request_ref[...] = scaled.astype(I32).reshape(dev_count, 1, width)


def coordinates(index, lon_count):
    return (index // lon_count, lax.rem(index, lon_count))


def my_index(lon_count):
    return lax.axis_index("lat") * lon_count + lax.axis_index("lon")


def greet_all(me, dev_count, lon_count):
    barrier = pltpu.get_barrier_semaphore()

    @pl.loop(1, dev_count)
    def _(d):
        other = lax.rem(me + d, dev_count)
        pl.semaphore_signal(
            barrier, inc=1, device_id=coordinates(other, lon_count), device_id_type=MESH
        )

    return barrier


def all_of(ref, sem):
    blocks = ref.at[pl.ds(0, ref.shape[0] - 1)]
    pltpu.make_async_copy(blocks, blocks, sem).wait()


def scatter_blocks(me, lon_count, given, taken, send, recv, before=None):
    dev_count = given.shape[0]

    @pl.loop(1, dev_count)
    def _(d):
        other = lax.rem(me + d, dev_count)
        if before is not None:
            before(other)
        pltpu.make_async_remote_copy(
            src_ref=given.at[other],
            dst_ref=taken.at[me],
            send_sem=send,
            recv_sem=recv,
            device_id=coordinates(other, lon_count),
            device_id_type=MESH,
        ).start()

    if before is not None:
        before(me)
    taken[me] = given[me]


DIRECTIONS = [(a, b) for a in (-1, 0, 1) for b in (-1, 0, 1) if (a, b) != (0, 0)]


class Edges:
    def __init__(self, lat_count, lon_count, source, target, send, recv):
        self.lat_count, self.lon_count = lat_count, lon_count
        self.source, self.target, self.send, self.recv = source, target, send, recv
        self.lat, self.lon = lax.axis_index("lat"), lax.axis_index("lon")

    def there(self, a):
        return jnp.logical_and(self.lat + a >= 0, self.lat + a < self.lat_count)

    def device(self, a, b):
        return (self.lat + a, lax.rem(self.lon + b + self.lon_count, self.lon_count))

    def copy(self, n):
        def span(step, size):
            given = {-1: pl.ds(0, HALO), 0: pl.ds(0, size), 1: pl.ds(size - HALO, HALO)}[step]
            taken = {-1: pl.ds(HALO + size, HALO), 0: pl.ds(HALO, size), 1: pl.ds(0, HALO)}[step]
            return given, taken

        a, b = DIRECTIONS[n]
        given_rows, taken_rows = span(a, self.source.shape[0])
        given_cols, taken_cols = span(b, self.source.shape[1])
        return pltpu.make_async_remote_copy(
            src_ref=self.source.at[given_rows, given_cols],
            dst_ref=self.target.at[taken_rows, taken_cols],
            send_sem=self.send.at[n],
            recv_sem=self.recv.at[n],
            device_id=self.device(a, b),
            device_id_type=MESH,
        )

    def each(self, sign, act):
        for n, (a, b) in enumerate(DIRECTIONS):

            @pl.when(self.there(sign * a))
            def _(n=n):
                act(self.copy(n))

    def start(self):
        self.each(1, lambda copy: copy.start())

    def arrive(self):
        self.each(-1, lambda copy: copy.wait_recv())

    def sent(self):
        self.each(1, lambda copy: copy.wait_send())


def observe_kernel(
    cap,
    lat_count,
    lon_count,
    slot_ref,
    request_ref,
    background_ref,
    observed_ref,
    accept_ref,
    absorb_ref,
    sensitivity_ref,
    variance_ref,
    kappa_ref,
    asked_ref,
    departure_ref,
    pulled_ref,
    kappa_wide_ref,
    field,
    found,
    arrived,
    asked_smem,
    zeros,
    chosen,
    profile,
    slope,
    weight,
    absorb_wide,
    sens_log,
    sens_ln,
    depth,
    transmit,
    sums,
    adjoint,
    block_send,
    block_recv,
    edge_send,
    edge_recv,
    local_sems,
):
    dev_count = request_ref.shape[0]
    tile_cols = 64
    me = my_index(lon_count)
    barrier = greet_all(me, dev_count, lon_count)

    height, breadth, levels = kappa_ref.shape
    edges = Edges(lat_count, lon_count, kappa_ref, kappa_wide_ref, edge_send, edge_recv)
    own = pltpu.make_async_copy(
        kappa_ref, kappa_wide_ref.at[pl.ds(HALO, height), pl.ds(HALO, breadth)], local_sems.at[0]
    )
    own.start()
    zeros[...] = jnp.zeros(zeros.shape, F32)

    def blank(a):
        rows = pl.ds(0, HALO) if a < 0 else pl.ds(HALO + height, HALO)
        return pltpu.make_async_copy(zeros, kappa_wide_ref.at[rows], local_sems.at[1])

    for a in (-1, 1):

        @pl.when(jnp.logical_not(edges.there(a)))
        def _(a=a):
            blank(a).start()
            blank(a).wait()

    chunk = 256

    @pl.loop(0, background_ref.shape[0] // chunk)
    def _(j):
        at = pl.ds(pl.multiple_of(j * chunk, chunk), chunk)
        field[at, :] = background_ref[at, :].astype(F32)

    slots = dev_count * cap
    feet, channels = observed_ref.shape
    groups = feet // LANES
    parts = channels // SUB

    wide = lambda row: jnp.swapaxes(jnp.broadcast_to(row, (LANES, channels)), 0, 1)
    sens = wide(sensitivity_ref[...])
    sens_log[...] = sens * LOG2E
    sens_ln[...] = sens * LN2

    absorb_t = jnp.swapaxes(absorb_ref[...] * (-LOG2E), 0, 1)

    @pl.loop(0, levels // SUB)
    def _(j):
        turned = pltpu.roll(absorb_t, lax.rem(levels - j * SUB, levels), 1)
        for i in range(SUB):
            absorb_wide[j * SUB + i] = jnp.broadcast_to(turned[:, i : i + 1], (channels, LANES))

    pl.semaphore_wait(barrier, dev_count - 1)
    scatter_blocks(
        me, lon_count, request_ref, asked_ref, block_send.at[0], block_recv.at[0]
    )
    edges.start()

    block = 256 if slots % 256 == 0 else slots

    @pl.loop(0, slots // block)
    def _(j):
        first = pl.multiple_of(j * block, block)
        here = lax.broadcasted_iota(I32, (block, feet), 0) + first == slot_ref[...]
        chosen[pl.ds(first, block), :] = here.astype(F32).astype(BF16)

    for g in range(groups):
        at = pl.ds(g * LANES, LANES)
        accepted = accept_ref[at, :].astype(F32) * variance_ref[...]
        weight[:, at] = jnp.swapaxes(accepted, 0, 1)

    level = lax.broadcasted_iota(I32, (levels, levels * SUB), 0)
    source = lax.broadcasted_iota(I32, (levels, levels * SUB), 1) // SUB
    same = (level == source).astype(F32)
    fall = (level == source + 1).astype(F32) - jnp.where(level == levels - 1, 0.0, same)
    same = same.astype(BF16)
    fall = fall.astype(BF16)

    all_of(asked_ref, block_recv.at[0])
    to_smem = pltpu.make_async_copy(asked_ref, asked_smem, local_sems.at[1])
    to_smem.start()
    to_smem.wait()

    def gather(source):
        for r in range(cap):
            at = asked_smem[source, 0, r]
            total = None
            for k, offset in enumerate((0, 1, tile_cols, tile_cols + 1)):
                share = asked_smem[source, 0, (k + 1) * cap + r].astype(F32)
                term = share * field[pl.ds(at + offset, 1), :]
                total = term if total is None else total + term
            found[source, r : r + 1, :] = total * (1.0 / FIXED)

    scatter_blocks(
        me, lon_count, found, arrived, block_send.at[1], block_recv.at[1], gather
    )
    all_of(arrived, block_recv.at[1])
    all_of(found, block_send.at[1])

    arrived_t = jnp.swapaxes(arrived[...].reshape(slots, levels), 0, 1)
    high, middle, low = pieces(arrived_t)
    plain = ((1,), (0,))
    mine = dot(high, chosen[...], plain) + dot(middle, chosen[...], plain) + dot(low, chosen[...], plain)
    below = jnp.concatenate([mine[1:, :], mine[levels - 1 :, :]], axis=0)
    for g in range(groups):
        at = slice(g * LANES, (g + 1) * LANES)
        profile[g] = mine[:, at]
        slope[g] = below[:, at] - mine[:, at]

    for g in range(groups):
        at = pl.ds(g * LANES, LANES)

        def descend(l, carry):
            p = profile[g, pl.ds(l, 1), :]
            q = slope[g, pl.ds(l, 1), :]
            out = []
            for c in range(parts):
                rows = slice(c * SUB, (c + 1) * SUB)
                optical, evolved = carry[c]
                layer = absorb_wide[l, rows, :] * jnp.exp2(sens_log[rows, :] * p)
                optical = optical + layer
                passed = jnp.exp2(optical)
                depth[l, rows, :] = layer
                transmit[l, rows, :] = passed
                out.append((optical, evolved + q * passed))
            return tuple(out)

        zero = jnp.zeros((SUB, LANES), F32)
        done = lax.fori_loop(0, levels, descend, ((zero, zero),) * parts, unroll=4)
        top = profile[g, 0:1, :]
        observed_t = jnp.swapaxes(observed_ref[at, :], 0, 1)
        departed = []
        pulls = []
        for c in range(parts):
            rows = slice(c * SUB, (c + 1) * SUB)
            part = observed_t[rows, :] - (done[c][1] + top)
            departed.append(part)
            pulls.append(-(weight[rows, at] * part))
        departure_ref[at, :] = jnp.swapaxes(jnp.concatenate(departed, axis=0), 0, 1)
        whole = pulls[0]
        for c in range(1, parts):
            whole = whole + pulls[c]
        whole = jnp.sum(whole, axis=0, keepdims=True)
        transmit_pull = tuple(pulls)

        def ascend(step, carry):
            l = levels - 1 - step
            q = slope[g, pl.ds(l, 1), :]
            out = []
            passed_sum = None
            layer_sum = None
            for c in range(parts):
                rows = slice(c * SUB, (c + 1) * SUB)
                pulled = transmit_pull[c] * transmit[l, rows, :]
                rest = carry[c] + q * pulled
                through = sens_ln[rows, :] * (depth[l, rows, :] * rest)
                passed_sum = pulled if c == 0 else passed_sum + pulled
                layer_sum = through if c == 0 else layer_sum + through
                out.append(rest)
            at_l = pl.ds(pl.multiple_of(l * SUB, SUB), SUB)
            sums[0, at_l, :] = passed_sum
            sums[1, at_l, :] = layer_sum
            return tuple(out)

        lax.fori_loop(0, levels, ascend, (zero,) * parts, unroll=4)
        total = None
        for matrix, index in ((fall, 0), (same, 1)):
            for piece in pieces(sums[index]):
                term = dot(matrix, piece, plain)
                total = term if total is None else total + term
        first = lax.broadcasted_iota(I32, (levels, LANES), 0) == 0
        adjoint[:, at] = total + jnp.where(first, whole, 0.0)

    parts_adjoint = pieces(adjoint[...])

    @pl.loop(0, slots // block)
    def _(j):
        rows = pl.ds(pl.multiple_of(j * block, block), block)
        total = None
        for piece in parts_adjoint:
            term = dot(chosen[rows, :], piece, ((1,), (1,)))
            total = term if total is None else total + term
        found[pl.ds(pl.multiple_of(j * (block // cap), block // cap), block // cap)] = total.reshape(
            block // cap, cap, levels
        )


    scatter_blocks(me, lon_count, found, pulled_ref, block_send.at[2], block_recv.at[2])
    own.wait()
    edges.sent()
    edges.arrive()
    all_of(request_ref, block_send.at[0])
    all_of(found, block_send.at[2])
    all_of(pulled_ref, block_recv.at[2])


def spread_kernel(cap, asked_ref, arrived_ref, raw_ref, other):
    tile_cols = 64
    cells, levels = raw_ref.shape
    chunk = 256

    @pl.loop(0, cells // chunk)
    def _(j):
        at = pl.ds(pl.multiple_of(j * chunk, chunk), chunk)
        raw_ref[at, :] = jnp.zeros((chunk, levels), F32)
        other[at, :] = jnp.zeros((chunk, levels), F32)

    @pl.loop(0, asked_ref.shape[0])
    def _(source):
        for r in range(0, cap, 2):
            for total, row in ((raw_ref, r), (other, r + 1)):
                at = asked_ref[source, 0, row]
                value = arrived_ref[source, row : row + 1, :]
                sites = [pl.ds(at + o, 1) for o in (0, 1, tile_cols, tile_cols + 1)]
                fresh = []
                for k in range(4):
                    share = asked_ref[source, 0, (k + 1) * cap + row].astype(F32)
                    fresh.append(total[sites[k], :] + share * value)
                for k in range(4):
                    total[sites[k], :] = fresh[k]

    @pl.loop(0, cells // chunk)
    def _(j):
        at = pl.ds(pl.multiple_of(j * chunk, chunk), chunk)
        raw_ref[at, :] = (raw_ref[at, :] + other[at, :]) * (-1.0 / FIXED)


def diffuse_kernel(
    lat_count,
    lon_count,
    raw_ref,
    kappa_ref,
    out_ref,
    field_in,
    kappa_in,
    field,
    east,
    south,
    local_sems,
    send_sems,
    recv_sems,
):
    height, breadth, levels = raw_ref.shape
    tall = height + 2 * HALO
    count = (breadth + 2 * HALO) // SUB
    edges = Edges(lat_count, lon_count, raw_ref, field_in, send_sems, recv_sems)
    is_first = edges.lat == 0
    is_last = edges.lat == lat_count - 1

    barrier = pltpu.get_barrier_semaphore()
    for a, b in DIRECTIONS:

        @pl.when(edges.there(a))
        def _(a=a, b=b):
            pl.semaphore_signal(
                barrier, inc=1, device_id=edges.device(a, b), device_id_type=MESH
            )

    centre = (pl.ds(HALO, height), pl.ds(HALO, breadth))
    kappa_copy = pltpu.make_async_copy(kappa_ref, kappa_in, local_sems.at[0])
    kappa_copy.start()
    own = pltpu.make_async_copy(raw_ref, field_in.at[centre], local_sems.at[1])
    own.start()

    zero_rows = jnp.zeros((HALO, breadth + 2 * HALO, levels), F32)
    flat_rows = jnp.zeros((HALO, count, SUB, levels), F32)

    @pl.when(is_first)
    def _():
        field_in[pl.ds(0, HALO)] = zero_rows
        field[pl.ds(0, HALO)] = flat_rows

    @pl.when(is_last)
    def _():
        field_in[pl.ds(HALO + height, HALO)] = zero_rows
        field[pl.ds(HALO + height, HALO)] = flat_rows

    neighbours = 8 - 3 * is_first.astype(I32) - 3 * is_last.astype(I32)
    pl.semaphore_wait(barrier, neighbours)
    edges.start()
    kappa_copy.wait()

    def strided(ref, r):
        return tuple(ref[r, pl.ds(i, SUB, stride=count), :] for i in range(count))

    def later(x):
        return pltpu.roll(x, SUB - 1, 0)

    def sooner(x):
        return pltpu.roll(x, 1, 0)

    def conduct(r, here):
        below = strided(kappa_in, jnp.minimum(r + 1, tall - 1))
        for i in range(count):
            beside = here[i + 1] if i + 1 < count else later(here[0])
            east[r, i] = 0.5 * (here[i] + beside)
            south[r, i] = 0.5 * (here[i] + below[i])
        return below

    lax.fori_loop(0, tall, conduct, strided(kappa_in, 0))
    own.wait()
    edges.arrive()

    def plain(ref, r):
        return tuple(ref[r, i] for i in range(count))

    for step in range(1, STEPS + 1):
        low = jnp.where(is_first, HALO, step)
        high = jnp.where(is_last, HALO + height, tall - step)
        if step == 1:
            load = functools.partial(strided, field_in)
        else:
            load = functools.partial(plain, field)

        def relax(r, carry, load=load, step=step):
            here, above = carry
            below = load(r + 1)
            down = [south[r, i] * (below[i] - here[i]) for i in range(count)]
            right = []
            for i in range(count):
                beside = here[i + 1] if i + 1 < count else later(here[0])
                right.append(east[r, i] * (beside - here[i]))
            for i in range(count):
                left = right[i - 1] if i > 0 else sooner(right[count - 1])
                new = here[i] + ((right[i] - left) + (down[i] - above[i]))
                if step == STEPS:
                    field_in[r, pl.ds(i, SUB, stride=count), :] = new
                else:
                    field[r, i] = new
            return below, tuple(down)

        before = load(low - 1)
        here = load(low)
        above = tuple(south[low - 1, i] * (here[i] - before[i]) for i in range(count))
        lax.fori_loop(low, high, relax, (here, above))

    result = pltpu.make_async_copy(field_in.at[centre], out_ref, local_sems.at[0])
    result.start()
    edges.sent()
    result.wait()


def local(
    lat_count,
    lon_count,
    background,
    diffusivity,
    tile_index,
    anchor,
    weights,
    observed,
    accept,
    absorb,
    sensitivity,
    inverse_variance,
):
    dev_count = lat_count * lon_count
    feet, channels = observed.shape
    cap = max(2, 2 * feet // dev_count)
    height, breadth, levels = background.shape
    slots = dev_count * cap
    width = -(-5 * cap // LANES) * LANES
    shape = jax.ShapeDtypeStruct
    params = functools.partial(pltpu.CompilerParams, vmem_limit_bytes=VMEM_BYTES)
    dma = pltpu.SemaphoreType.DMA

    slot, request = pl.pallas_call(
        functools.partial(request_kernel, cap),
        out_shape=(shape((1, feet), I32), shape((dev_count, 1, width), I32)),
        in_specs=[VMEM_SPEC] * 3,
        out_specs=(VMEM_SPEC, VMEM_SPEC),
        compiler_params=params(),
        name="request",
    )(tile_index.reshape(1, feet), anchor.reshape(1, feet), weights.T)

    wide = (height + 2 * HALO, breadth + 2 * HALO, levels)
    asked, departure, pulled, kappa_wide = pl.pallas_call(
        functools.partial(observe_kernel, cap, lat_count, lon_count),
        out_shape=(
            shape((dev_count, 1, width), I32),
            shape((feet, channels), F32),
            shape((dev_count, cap, levels), F32),
            shape(wide, F32),
        ),
        in_specs=[VMEM_SPEC] * 8 + [ANY_SPEC],
        out_specs=(VMEM_SPEC, VMEM_SPEC, VMEM_SPEC, ANY_SPEC),
        scratch_shapes=[
            pltpu.VMEM((height * breadth, levels), F32),
            pltpu.VMEM((dev_count, cap, levels), F32),
            pltpu.VMEM((dev_count, cap, levels), F32),
            pltpu.SMEM((dev_count, 1, width), I32),
            pltpu.VMEM((HALO,) + wide[1:], F32),
            pltpu.VMEM((slots, feet), BF16),
            pltpu.VMEM((feet // LANES, levels, LANES), F32),
            pltpu.VMEM((feet // LANES, levels, LANES), F32),
            pltpu.VMEM((channels, feet), F32),
            pltpu.VMEM((levels, channels, LANES), F32),
            pltpu.VMEM((channels, LANES), F32),
            pltpu.VMEM((channels, LANES), F32),
            pltpu.VMEM((levels, channels, LANES), F32),
            pltpu.VMEM((levels, channels, LANES), F32),
            pltpu.VMEM((2, levels * SUB, LANES), F32),
            pltpu.VMEM((levels, feet), F32),
            dma((3,)),
            dma((3,)),
            dma((8,)),
            dma((8,)),
            dma((2,)),
        ],
        compiler_params=params(collective_id=0, has_side_effects=True),
        name="observe",
    )(
        slot,
        request,
        background.reshape(height * breadth, levels),
        observed,
        accept,
        absorb,
        sensitivity.reshape(1, channels),
        inverse_variance.reshape(1, channels),
        diffusivity,
    )

    raw = pl.pallas_call(
        functools.partial(spread_kernel, cap),
        out_shape=shape((height * breadth, levels), F32),
        in_specs=[SMEM_SPEC, VMEM_SPEC],
        out_specs=VMEM_SPEC,
        scratch_shapes=[pltpu.VMEM((height * breadth, levels), F32)],
        compiler_params=params(),
        name="spread",
    )(asked, pulled)

    turned = (height + 2 * HALO, (breadth + 2 * HALO) // SUB, SUB, levels)
    increment = pl.pallas_call(
        functools.partial(diffuse_kernel, lat_count, lon_count),
        out_shape=shape((height, breadth, levels), F32),
        in_specs=[ANY_SPEC, ANY_SPEC],
        out_specs=ANY_SPEC,
        scratch_shapes=[
            pltpu.VMEM(wide, F32),
            pltpu.VMEM(wide, F32),
            pltpu.VMEM(turned, F32),
            pltpu.VMEM(turned, F32),
            pltpu.VMEM(turned, F32),
            dma((2,)),
            dma((8,)),
            dma((8,)),
        ],
        compiler_params=params(collective_id=1, has_side_effects=True),
        name="diffuse",
    )(raw.reshape(height, breadth, levels), kappa_wide)
    return (departure, increment)


def solution(mesh):
    in_specs = (
        P("lat", "lon", None),
        P("lat", "lon", None),
        P(("lat", "lon"), None),
        P(("lat", "lon")),
        P(("lat", "lon"), None),
        P(("lat", "lon"), None),
        P(("lat", "lon"), None),
        P(),
        P(),
        P(),
    )
    out_specs = (P(("lat", "lon"), None), P("lat", "lon", None))
    return jax.shard_map(
        functools.partial(local, mesh.shape["lat"], mesh.shape["lon"]),
        mesh=mesh,
        in_specs=in_specs,
        out_specs=out_specs,
        check_vma=False,
    )
```

```python
import functools

import jax
import jax.numpy as jnp
from jax import lax
from jax.experimental import pallas as pl
from jax.experimental.pallas import tpu as pltpu
from jax.sharding import PartitionSpec as P

STEPS = 8
HALO = 8
SUB = 8
LANES = 128
LOG2E = 1.4426950408889634
LN2 = 0.6931471805599453
FIXED = 2.0**30
F32 = jnp.float32
BF16 = jnp.bfloat16
I32 = jnp.int32
MESH = pl.DeviceIdType.MESH
VMEM_SPEC = pl.BlockSpec(memory_space=pltpu.VMEM)
SMEM_SPEC = pl.BlockSpec(memory_space=pltpu.SMEM)
ANY_SPEC = pl.BlockSpec(memory_space=pl.ANY)
VMEM_BYTES = 60 * 2**20


def pieces(x):
    high = x.astype(BF16)
    rest = x - high.astype(F32)
    middle = rest.astype(BF16)
    low = (rest - middle.astype(F32)).astype(BF16)
    return high, middle, low


def dot(a, b, contract):
    return lax.dot_general(a, b, (contract, ((), ())), preferred_element_type=F32)


def request_kernel(cap, tile_ref, anchor_ref, weights_ref, slot_ref, request_ref):
    dev_count, _, width = request_ref.shape
    feet = tile_ref.shape[1]
    tile = tile_ref[...]
    named = lax.broadcasted_iota(I32, (dev_count, feet), 0) == tile
    onehot = named.astype(F32).astype(BF16)
    before = (
        lax.broadcasted_iota(I32, (feet, feet), 0) < lax.broadcasted_iota(I32, (feet, feet), 1)
    )
    earlier = dot(onehot, before.astype(F32).astype(BF16), ((1,), (0,)))
    rank = jnp.sum(jnp.where(named, earlier, 0.0), axis=0, keepdims=True).astype(I32)
    slot_ref[...] = tile * cap + rank
    anchor = anchor_ref[...]
    row = ((anchor.astype(F32) + 0.5) * (1.0 / 63.0)).astype(I32)
    base = (anchor + row).astype(F32)
    weights = weights_ref[...]
    shares = weights / jnp.sum(weights, axis=0, keepdims=True)
    place = lax.broadcasted_iota(I32, (cap, feet), 0) == rank
    fields = [base] + [shares[k : k + 1, :] for k in range(4)]
    rows = [jnp.where(place, field, 0.0) for field in fields]
    if width > 5 * cap:
        rows.append(jnp.zeros((width - 5 * cap, feet), F32))
    packed = jnp.concatenate(rows, axis=0)
    high, middle, low = pieces(packed)
    last = ((1,), (1,))
    message = dot(onehot, high, last) + dot(onehot, middle, last) + dot(onehot, low, last)
    scaled = jnp.where(
        lax.broadcasted_iota(I32, (dev_count, width), 1) < cap, message, message * FIXED
    )
    request_ref[...] = scaled.astype(I32).reshape(dev_count, 1, width)


def coordinates(index, lon_count):
    return (index // lon_count, lax.rem(index, lon_count))


def my_index(lon_count):
    return lax.axis_index("lat") * lon_count + lax.axis_index("lon")


def greet_all(me, dev_count, lon_count):
    barrier = pltpu.get_barrier_semaphore()

    @pl.loop(1, dev_count)
    def _(d):
        other = lax.rem(me + d, dev_count)
        pl.semaphore_signal(
            barrier, inc=1, device_id=coordinates(other, lon_count), device_id_type=MESH
        )

    return barrier


def all_of(ref, sem):
    blocks = ref.at[pl.ds(0, ref.shape[0] - 1)]
    pltpu.make_async_copy(blocks, blocks, sem).wait()


def scatter_blocks(me, lon_count, given, taken, send, recv, before=None):
    dev_count = given.shape[0]

    @pl.loop(1, dev_count)
    def _(d):
        other = lax.rem(me + d, dev_count)
        if before is not None:
            before(other)
        pltpu.make_async_remote_copy(
            src_ref=given.at[other],
            dst_ref=taken.at[me],
            send_sem=send,
            recv_sem=recv,
            device_id=coordinates(other, lon_count),
            device_id_type=MESH,
        ).start()

    if before is not None:
        before(me)
    taken[me] = given[me]


DIRECTIONS = [(a, b) for a in (-1, 0, 1) for b in (-1, 0, 1) if (a, b) != (0, 0)]


class Edges:
    def __init__(self, lat_count, lon_count, source, target, send, recv, size=None):
        self.lat_count, self.lon_count = lat_count, lon_count
        self.source, self.target, self.send, self.recv = source, target, send, recv
        self.size = source.shape[:2] if size is None else size
        self.lat, self.lon = lax.axis_index("lat"), lax.axis_index("lon")

    def there(self, a):
        return jnp.logical_and(self.lat + a >= 0, self.lat + a < self.lat_count)

    def device(self, a, b):
        return (self.lat + a, lax.rem(self.lon + b + self.lon_count, self.lon_count))

    def copy(self, n, band=None):
        def span(step, size):
            given = {-1: pl.ds(0, HALO), 0: pl.ds(0, size), 1: pl.ds(size - HALO, HALO)}[step]
            taken = {-1: pl.ds(HALO + size, HALO), 0: pl.ds(HALO, size), 1: pl.ds(0, HALO)}[step]
            return given, taken

        a, b = DIRECTIONS[n]
        given_rows, taken_rows = span(a, self.size[0])
        given_cols, taken_cols = span(b, self.size[1])
        if band is not None:
            given_rows = pl.ds(band * HALO, HALO)
            taken_rows = pl.ds(HALO + band * HALO, HALO)
        return pltpu.make_async_remote_copy(
            src_ref=self.source.at[given_rows, given_cols],
            dst_ref=self.target.at[taken_rows, taken_cols],
            send_sem=self.send.at[n],
            recv_sem=self.recv.at[n],
            device_id=self.device(a, b),
            device_id_type=MESH,
        )

    def each(self, sign, act, which=lambda a: True):
        for n, (a, b) in enumerate(DIRECTIONS):
            if not which(a):
                continue

            @pl.when(self.there(sign * a))
            def _(n=n):
                act(self.copy(n))

    def start(self, which=lambda a: True):
        self.each(1, lambda copy: copy.start(), which)

    def arrive(self):
        self.each(-1, lambda copy: copy.wait_recv())

    def sent(self):
        self.each(1, lambda copy: copy.wait_send())


def observe_kernel(
    cap,
    lat_count,
    lon_count,
    slot_ref,
    request_ref,
    background_ref,
    observed_ref,
    accept_ref,
    absorb_ref,
    sensitivity_ref,
    variance_ref,
    kappa_ref,
    departure_ref,
    increment_ref,
    asked_ref,
    pulled_ref,
    columns,
    found,
    arrived,
    asked_smem,
    chosen,
    profile,
    slope,
    weight,
    absorb_wide,
    sens_log,
    sens_ln,
    depth,
    transmit,
    sums,
    adjoint,
    wanted,
    upper,
    lower,
    row_of,
    terms,
    sharing,
    field_in,
    kappa_in,
    field,
    east,
    south,
    block_send,
    block_recv,
    edge_send,
    edge_recv,
    local_sems,
):
    dev_count = request_ref.shape[0]
    tile_cols = 64
    me = my_index(lon_count)
    barrier = greet_all(me, dev_count, lon_count)

    height, breadth, levels = kappa_ref.shape
    tall = height + 2 * HALO
    count = (breadth + 2 * HALO) // SUB
    centre = (pl.ds(HALO, height), pl.ds(HALO, breadth))
    kappa_edges = Edges(
        lat_count, lon_count, kappa_ref, kappa_in, edge_send.at[0], edge_recv.at[0]
    )
    kappa_own = pltpu.make_async_copy(kappa_ref, kappa_in.at[centre], local_sems.at[0])
    kappa_own.start()
    is_first = kappa_edges.lat == 0
    is_last = kappa_edges.lat == lat_count - 1
    for outside, rows in ((is_first, pl.ds(0, HALO)), (is_last, pl.ds(HALO + height, HALO))):

        @pl.when(outside)
        def _(rows=rows):
            kappa_in[rows] = jnp.zeros((HALO,) + kappa_in.shape[1:], F32)
            field_in[rows] = jnp.zeros((HALO,) + field_in.shape[1:], F32)
            field[rows] = jnp.zeros((HALO,) + field.shape[1:], F32)

    chunk = 256

    @pl.loop(0, background_ref.shape[0] // chunk)
    def _(j):
        at = pl.ds(pl.multiple_of(j * chunk, chunk), chunk)
        columns[at, :] = background_ref[at, :].astype(F32)

    slots = dev_count * cap
    feet, channels = observed_ref.shape
    groups = feet // LANES
    parts = channels // SUB

    wide = lambda row: jnp.swapaxes(jnp.broadcast_to(row, (LANES, channels)), 0, 1)
    sens = wide(sensitivity_ref[...])
    sens_log[...] = sens * LOG2E
    sens_ln[...] = sens * LN2

    absorb_t = jnp.swapaxes(absorb_ref[...] * (-LOG2E), 0, 1)

    @pl.loop(0, levels // SUB)
    def _(j):
        turned = pltpu.roll(absorb_t, lax.rem(levels - j * SUB, levels), 1)
        for i in range(SUB):
            absorb_wide[j * SUB + i] = jnp.broadcast_to(turned[:, i : i + 1], (channels, LANES))

    pl.semaphore_wait(barrier, dev_count - 1)
    scatter_blocks(
        me, lon_count, request_ref, asked_ref, block_send.at[0], block_recv.at[0]
    )
    kappa_edges.start()

    block = 256 if slots % 256 == 0 else slots

    @pl.loop(0, slots // block)
    def _(j):
        first = pl.multiple_of(j * block, block)
        here = lax.broadcasted_iota(I32, (block, feet), 0) + first == slot_ref[...]
        chosen[pl.ds(first, block), :] = here.astype(F32).astype(BF16)

    for g in range(groups):
        at = pl.ds(g * LANES, LANES)
        accepted = accept_ref[at, :].astype(F32) * variance_ref[...]
        weight[:, at] = jnp.swapaxes(accepted, 0, 1)

    level = lax.broadcasted_iota(I32, (levels, levels * SUB), 0)
    source = lax.broadcasted_iota(I32, (levels, levels * SUB), 1) // SUB
    same = (level == source).astype(F32)
    fall = (level == source + 1).astype(F32) - jnp.where(level == levels - 1, 0.0, same)
    same = same.astype(BF16)
    fall = fall.astype(BF16)

    all_of(asked_ref, block_recv.at[0])
    to_smem = pltpu.make_async_copy(asked_ref, asked_smem, local_sems.at[1])
    to_smem.start()
    to_smem.wait()

    def gather(source):
        for r in range(cap):
            at = asked_smem[source, 0, r]
            total = None
            for k, offset in enumerate((0, 1, tile_cols, tile_cols + 1)):
                share = asked_smem[source, 0, (k + 1) * cap + r].astype(F32)
                term = share * columns[pl.ds(at + offset, 1), :]
                total = term if total is None else total + term
            found[source, r : r + 1, :] = total * (1.0 / FIXED)

    scatter_blocks(
        me, lon_count, found, arrived, block_send.at[1], block_recv.at[1], gather
    )
    all_of(arrived, block_recv.at[1])
    all_of(found, block_send.at[1])

    arrived_t = jnp.swapaxes(arrived[...].reshape(slots, levels), 0, 1)
    high, middle, low = pieces(arrived_t)
    plain = ((1,), (0,))
    mine = dot(high, chosen[...], plain) + dot(middle, chosen[...], plain) + dot(low, chosen[...], plain)
    below = jnp.concatenate([mine[1:, :], mine[levels - 1 :, :]], axis=0)
    for g in range(groups):
        at = slice(g * LANES, (g + 1) * LANES)
        profile[g] = mine[:, at]
        slope[g] = below[:, at] - mine[:, at]

    for g in range(groups):
        at = pl.ds(g * LANES, LANES)

        def descend(l, carry):
            p = profile[g, pl.ds(l, 1), :]
            q = slope[g, pl.ds(l, 1), :]
            out = []
            for c in range(parts):
                rows = slice(c * SUB, (c + 1) * SUB)
                optical, evolved = carry[c]
                layer = absorb_wide[l, rows, :] * jnp.exp2(sens_log[rows, :] * p)
                optical = optical + layer
                passed = jnp.exp2(optical)
                depth[l, rows, :] = layer
                transmit[l, rows, :] = passed
                out.append((optical, evolved + q * passed))
            return tuple(out)

        zero = jnp.zeros((SUB, LANES), F32)
        done = lax.fori_loop(0, levels, descend, ((zero, zero),) * parts, unroll=4)
        top = profile[g, 0:1, :]
        observed_t = jnp.swapaxes(observed_ref[at, :], 0, 1)
        departed = []
        pulls = []
        for c in range(parts):
            rows = slice(c * SUB, (c + 1) * SUB)
            part = observed_t[rows, :] - (done[c][1] + top)
            departed.append(part)
            pulls.append(-(weight[rows, at] * part))
        departure_ref[at, :] = jnp.swapaxes(jnp.concatenate(departed, axis=0), 0, 1)
        whole = pulls[0]
        for c in range(1, parts):
            whole = whole + pulls[c]
        whole = jnp.sum(whole, axis=0, keepdims=True)
        transmit_pull = tuple(pulls)

        def ascend(step, carry):
            l = levels - 1 - step
            q = slope[g, pl.ds(l, 1), :]
            out = []
            passed_sum = None
            layer_sum = None
            for c in range(parts):
                rows = slice(c * SUB, (c + 1) * SUB)
                pulled = transmit_pull[c] * transmit[l, rows, :]
                rest = carry[c] + q * pulled
                through = sens_ln[rows, :] * (depth[l, rows, :] * rest)
                passed_sum = pulled if c == 0 else passed_sum + pulled
                layer_sum = through if c == 0 else layer_sum + through
                out.append(rest)
            at_l = pl.ds(pl.multiple_of(l * SUB, SUB), SUB)
            sums[0, at_l, :] = passed_sum
            sums[1, at_l, :] = layer_sum
            return tuple(out)

        lax.fori_loop(0, levels, ascend, (zero,) * parts, unroll=4)
        total = None
        for matrix, index in ((fall, 0), (same, 1)):
            for piece in pieces(sums[index]):
                term = dot(matrix, piece, plain)
                total = term if total is None else total + term
        first = lax.broadcasted_iota(I32, (levels, LANES), 0) == 0
        adjoint[:, at] = total + jnp.where(first, whole, 0.0)

    parts_adjoint = pieces(adjoint[...])

    @pl.loop(0, slots // block)
    def _(j):
        rows = pl.ds(pl.multiple_of(j * block, block), block)
        total = None
        for piece in parts_adjoint:
            term = dot(chosen[rows, :], piece, ((1,), (1,)))
            total = term if total is None else total + term
        found[pl.ds(pl.multiple_of(j * (block // cap), block // cap), block // cap)] = total.reshape(
            block // cap, cap, levels
        )


    scatter_blocks(me, lon_count, found, pulled_ref, block_send.at[2], block_recv.at[2])

    @pl.loop(0, dev_count)
    def _(source):
        wanted[pl.ds(source, 1), :] = asked_ref[source]

    asked_t = jnp.swapaxes(wanted[...], 0, 1)
    column = lax.broadcasted_iota(I32, (breadth, dev_count), 0)
    shift = breadth.bit_length() - 1
    for r in range(cap):
        base = asked_t[r : r + 1, :]
        base_row = lax.shift_right_logical(base, shift)
        base_col = base - lax.shift_left(base_row, shift)
        shares = [
            asked_t[(k + 1) * cap + r : (k + 1) * cap + r + 1, :].astype(F32) * (1.0 / FIXED)
            for k in range(4)
        ]
        at = slice(r * dev_count, (r + 1) * dev_count)
        row_of[:, at] = base_row.astype(F32)
        for target, first, second in ((upper, shares[0], shares[1]), (lower, shares[2], shares[3])):
            taken = jnp.where(column == base_col, first, 0.0)
            taken = jnp.where(column == base_col + 1, second, taken)
            high = taken.astype(BF16)
            target[0:breadth, at] = high
            target[breadth : 2 * breadth, at] = (taken - high.astype(F32)).astype(BF16)

    kappa_own.wait()
    kappa_edges.sent()
    kappa_edges.arrive()

    def strided(ref, r):
        return tuple(ref[r, pl.ds(i, SUB, stride=count), :] for i in range(count))

    def later(x):
        return pltpu.roll(x, SUB - 1, 0)

    def sooner(x):
        return pltpu.roll(x, 1, 0)

    def conduct(r, here):
        below = strided(kappa_in, jnp.minimum(r + 1, tall - 1))
        for i in range(count):
            beside = here[i + 1] if i + 1 < count else later(here[0])
            east[r, i] = 0.5 * (here[i] + beside)
            south[r, i] = 0.5 * (here[i] + below[i])
        return below

    lax.fori_loop(0, tall, conduct, strided(kappa_in, 0))

    all_of(request_ref, block_send.at[0])
    all_of(found, block_send.at[2])
    all_of(pulled_ref, block_recv.at[2])

    slot_rows = pulled_ref.reshape(slots, levels)
    for r in range(cap):
        pulled = slot_rows[pl.ds(r, dev_count, stride=cap), :]
        high = pulled.astype(BF16)
        at = slice(r * dev_count, (r + 1) * dev_count)
        terms[at, 0:levels] = high
        terms[at, levels : 2 * levels] = (pulled - high.astype(F32)).astype(BF16)

    edges = Edges(
        lat_count,
        lon_count,
        field_in.at[centre],
        field_in,
        edge_send.at[1],
        edge_recv.at[1],
        (height, breadth),
    )
    bands = height // HALO

    @pl.loop(0, bands)
    def _(turn):
        band = jnp.where(turn == 0, 0, jnp.where(turn == 1, bands - 1, turn - 1))
        for g in range(HALO):
            row = (band * HALO + g).astype(F32)
            in_upper = (row_of[...] == row).astype(F32).astype(BF16)
            in_lower = (row_of[...] == row - 1.0).astype(F32).astype(BF16)
            sharing[g * 2 * breadth : (g + 1) * 2 * breadth, :] = (
                upper[...] * in_upper + lower[...] * in_lower
            )
        product = dot(sharing[...], terms[...], ((1,), (0,)))
        for g in range(HALO):
            first = g * 2 * breadth
            second = first + breadth
            raw = (
                product[first:second, 0:levels]
                + product[first:second, levels : 2 * levels]
                + product[second : second + breadth, 0:levels]
            )
            field_in[HALO + band * HALO + g, pl.ds(HALO, breadth), :] = -raw
        for n, (a, b) in enumerate(DIRECTIONS):
            if a == 0:
                edges.copy(n, band).start()

        @pl.when(turn == 1)
        def _():
            edges.start(lambda a: a != 0)

    edges.arrive()
    edges.sent()

    def whole_rows(ref, r):
        return tuple(ref[r, i] for i in range(count))

    for step in range(1, STEPS + 1):
        low = jnp.where(is_first, HALO, step)
        high = jnp.where(is_last, HALO + height, tall - step)
        if step == 1:
            load = functools.partial(strided, field_in)
        else:
            load = functools.partial(whole_rows, field)

        def relax(r, carry, load=load, step=step):
            here, above = carry
            below = load(r + 1)
            down = [south[r, i] * (below[i] - here[i]) for i in range(count)]
            right = []
            for i in range(count):
                beside = here[i + 1] if i + 1 < count else later(here[0])
                right.append(east[r, i] * (beside - here[i]))
            for i in range(count):
                left = right[i - 1] if i > 0 else sooner(right[count - 1])
                new = here[i] + ((right[i] - left) + (down[i] - above[i]))
                if step == STEPS:
                    field_in[r, pl.ds(i, SUB, stride=count), :] = new
                else:
                    field[r, i] = new
            return below, tuple(down)

        before = load(low - 1)
        here = load(low)
        above = tuple(south[low - 1, i] * (here[i] - before[i]) for i in range(count))
        lax.fori_loop(low, high, relax, (here, above))

    result = pltpu.make_async_copy(field_in.at[centre], increment_ref, local_sems.at[0])
    result.start()
    result.wait()


def local(
    lat_count,
    lon_count,
    background,
    diffusivity,
    tile_index,
    anchor,
    weights,
    observed,
    accept,
    absorb,
    sensitivity,
    inverse_variance,
):
    dev_count = lat_count * lon_count
    feet, channels = observed.shape
    cap = max(2, 2 * feet // dev_count)
    height, breadth, levels = background.shape
    slots = dev_count * cap
    width = -(-5 * cap // LANES) * LANES
    shape = jax.ShapeDtypeStruct
    params = functools.partial(pltpu.CompilerParams, vmem_limit_bytes=VMEM_BYTES)
    dma = pltpu.SemaphoreType.DMA

    slot, request = pl.pallas_call(
        functools.partial(request_kernel, cap),
        out_shape=(shape((1, feet), I32), shape((dev_count, 1, width), I32)),
        in_specs=[VMEM_SPEC] * 3,
        out_specs=(VMEM_SPEC, VMEM_SPEC),
        compiler_params=params(),
        name="request",
    )(tile_index.reshape(1, feet), anchor.reshape(1, feet), weights.T)

    wide = (height + 2 * HALO, breadth + 2 * HALO, levels)
    turned = (wide[0], wide[1] // SUB, SUB, levels)
    departure, increment = pl.pallas_call(
        functools.partial(observe_kernel, cap, lat_count, lon_count),
        out_shape=(shape((feet, channels), F32), shape((height, breadth, levels), F32)),
        in_specs=[VMEM_SPEC] * 8 + [ANY_SPEC],
        out_specs=(VMEM_SPEC, ANY_SPEC),
        scratch_shapes=[
            pltpu.VMEM((dev_count, 1, width), I32),
            pltpu.VMEM((dev_count, cap, levels), F32),
            pltpu.VMEM((height * breadth, levels), F32),
            pltpu.VMEM((dev_count, cap, levels), F32),
            pltpu.VMEM((dev_count, cap, levels), F32),
            pltpu.SMEM((dev_count, 1, width), I32),
            pltpu.VMEM((slots, feet), BF16),
            pltpu.VMEM((feet // LANES, levels, LANES), F32),
            pltpu.VMEM((feet // LANES, levels, LANES), F32),
            pltpu.VMEM((channels, feet), F32),
            pltpu.VMEM((levels, channels, LANES), F32),
            pltpu.VMEM((channels, LANES), F32),
            pltpu.VMEM((channels, LANES), F32),
            pltpu.VMEM((levels, channels, LANES), F32),
            pltpu.VMEM((levels, channels, LANES), F32),
            pltpu.VMEM((2, levels * SUB, LANES), F32),
            pltpu.VMEM((levels, feet), F32),
            pltpu.VMEM((dev_count, width), I32),
            pltpu.VMEM((2 * breadth, slots), BF16),
            pltpu.VMEM((2 * breadth, slots), BF16),
            pltpu.VMEM((1, slots), F32),
            pltpu.VMEM((slots, 2 * levels), BF16),
            pltpu.VMEM((HALO * 2 * breadth, slots), BF16),
            pltpu.VMEM(wide, F32),
            pltpu.VMEM(wide, F32),
            pltpu.VMEM(turned, F32),
            pltpu.VMEM(turned, F32),
            pltpu.VMEM(turned, F32),
            dma((3,)),
            dma((3,)),
            dma((2, 8)),
            dma((2, 8)),
            dma((2,)),
        ],
        compiler_params=params(collective_id=0, has_side_effects=True),
        name="observe",
    )(
        slot,
        request,
        background.reshape(height * breadth, levels),
        observed,
        accept,
        absorb,
        sensitivity.reshape(1, channels),
        inverse_variance.reshape(1, channels),
        diffusivity,
    )

    return (departure, increment)


def solution(mesh):
    in_specs = (
        P("lat", "lon", None),
        P("lat", "lon", None),
        P(("lat", "lon"), None),
        P(("lat", "lon")),
        P(("lat", "lon"), None),
        P(("lat", "lon"), None),
        P(("lat", "lon"), None),
        P(),
        P(),
        P(),
    )
    out_specs = (P(("lat", "lon"), None), P("lat", "lon", None))
    return jax.shard_map(
        functools.partial(local, mesh.shape["lat"], mesh.shape["lon"]),
        mesh=mesh,
        in_specs=in_specs,
        out_specs=out_specs,
        check_vma=False,
    )
```

```python
import functools

import jax
import jax.numpy as jnp
from jax import lax
from jax.experimental import pallas as pl
from jax.experimental.pallas import tpu as pltpu
from jax.sharding import PartitionSpec as P

STEPS = 8
HALO = 8
SUB = 8
LANES = 128
LOG2E = 1.4426950408889634
LN2 = 0.6931471805599453
FIXED = 2.0**30
F32 = jnp.float32
BF16 = jnp.bfloat16
I32 = jnp.int32
MESH = pl.DeviceIdType.MESH
VMEM_SPEC = pl.BlockSpec(memory_space=pltpu.VMEM)
SMEM_SPEC = pl.BlockSpec(memory_space=pltpu.SMEM)
ANY_SPEC = pl.BlockSpec(memory_space=pl.ANY)
VMEM_BYTES = 60 * 2**20


def pieces(x):
    high = x.astype(BF16)
    rest = x - high.astype(F32)
    middle = rest.astype(BF16)
    low = (rest - middle.astype(F32)).astype(BF16)
    return high, middle, low


def dot(a, b, contract):
    return lax.dot_general(a, b, (contract, ((), ())), preferred_element_type=F32)


def request_kernel(cap, tile_ref, anchor_ref, weights_ref, slot_ref, request_ref):
    dev_count, _, width = request_ref.shape
    feet = tile_ref.shape[1]
    tile = tile_ref[...]
    named = lax.broadcasted_iota(I32, (dev_count, feet), 0) == tile
    onehot = named.astype(F32).astype(BF16)
    before = (
        lax.broadcasted_iota(I32, (feet, feet), 0) < lax.broadcasted_iota(I32, (feet, feet), 1)
    )
    earlier = dot(onehot, before.astype(F32).astype(BF16), ((1,), (0,)))
    rank = jnp.sum(jnp.where(named, earlier, 0.0), axis=0, keepdims=True).astype(I32)
    slot_ref[...] = tile * cap + rank
    anchor = anchor_ref[...]
    row = ((anchor.astype(F32) + 0.5) * (1.0 / 63.0)).astype(I32)
    base = (anchor + row).astype(F32)
    weights = weights_ref[...]
    shares = weights / jnp.sum(weights, axis=0, keepdims=True)
    place = lax.broadcasted_iota(I32, (cap, feet), 0) == rank
    fields = [base] + [shares[k : k + 1, :] for k in range(4)]
    rows = [jnp.where(place, field, 0.0) for field in fields]
    if width > 5 * cap:
        rows.append(jnp.zeros((width - 5 * cap, feet), F32))
    packed = jnp.concatenate(rows, axis=0)
    high, middle, low = pieces(packed)
    last = ((1,), (1,))
    message = dot(onehot, high, last) + dot(onehot, middle, last) + dot(onehot, low, last)
    scaled = jnp.where(
        lax.broadcasted_iota(I32, (dev_count, width), 1) < cap, message, message * FIXED
    )
    request_ref[...] = scaled.astype(I32).reshape(dev_count, 1, width)


def coordinates(index, lon_count):
    return (index // lon_count, lax.rem(index, lon_count))


def my_index(lon_count):
    return lax.axis_index("lat") * lon_count + lax.axis_index("lon")


def greet_all(me, dev_count, lon_count):
    barrier = pltpu.get_barrier_semaphore()

    @pl.loop(1, dev_count)
    def _(d):
        other = lax.rem(me + d, dev_count)
        pl.semaphore_signal(
            barrier, inc=1, device_id=coordinates(other, lon_count), device_id_type=MESH
        )

    return barrier


def all_of(ref, sem):
    blocks = ref.at[pl.ds(0, ref.shape[0] - 1)]
    pltpu.make_async_copy(blocks, blocks, sem).wait()


def scatter_blocks(me, lon_count, given, taken, send, recv, before=None):
    dev_count = given.shape[0]

    @pl.loop(1, dev_count)
    def _(d):
        other = lax.rem(me + d, dev_count)
        if before is not None:
            before(other)
        pltpu.make_async_remote_copy(
            src_ref=given.at[other],
            dst_ref=taken.at[me],
            send_sem=send,
            recv_sem=recv,
            device_id=coordinates(other, lon_count),
            device_id_type=MESH,
        ).start()

    if before is not None:
        before(me)
    taken[me] = given[me]


DIRECTIONS = [(a, b) for a in (-1, 0, 1) for b in (-1, 0, 1) if (a, b) != (0, 0)]


class Edges:
    def __init__(self, lat_count, lon_count, source, target, send, recv, size=None):
        self.lat_count, self.lon_count = lat_count, lon_count
        self.source, self.target, self.send, self.recv = source, target, send, recv
        self.size = source.shape[:2] if size is None else size
        self.lat, self.lon = lax.axis_index("lat"), lax.axis_index("lon")

    def there(self, a):
        return jnp.logical_and(self.lat + a >= 0, self.lat + a < self.lat_count)

    def device(self, a, b):
        return (self.lat + a, lax.rem(self.lon + b + self.lon_count, self.lon_count))

    def copy(self, n, band=None):
        def span(step, size):
            given = {-1: pl.ds(0, HALO), 0: pl.ds(0, size), 1: pl.ds(size - HALO, HALO)}[step]
            taken = {-1: pl.ds(HALO + size, HALO), 0: pl.ds(HALO, size), 1: pl.ds(0, HALO)}[step]
            return given, taken

        a, b = DIRECTIONS[n]
        given_rows, taken_rows = span(a, self.size[0])
        given_cols, taken_cols = span(b, self.size[1])
        if band is not None:
            given_rows = pl.ds(band * HALO, HALO)
            taken_rows = pl.ds(HALO + band * HALO, HALO)
        return pltpu.make_async_remote_copy(
            src_ref=self.source.at[given_rows, given_cols],
            dst_ref=self.target.at[taken_rows, taken_cols],
            send_sem=self.send.at[n],
            recv_sem=self.recv.at[n],
            device_id=self.device(a, b),
            device_id_type=MESH,
        )

    def each(self, sign, act, which=lambda a: True):
        for n, (a, b) in enumerate(DIRECTIONS):
            if not which(a):
                continue

            @pl.when(self.there(sign * a))
            def _(n=n):
                act(self.copy(n))

    def start(self, which=lambda a: True):
        self.each(1, lambda copy: copy.start(), which)

    def arrive(self):
        self.each(-1, lambda copy: copy.wait_recv())

    def sent(self):
        self.each(1, lambda copy: copy.wait_send())


def observe_kernel(
    cap,
    lat_count,
    lon_count,
    slot_ref,
    request_ref,
    background_ref,
    observed_ref,
    accept_ref,
    absorb_ref,
    sensitivity_ref,
    variance_ref,
    kappa_ref,
    departure_ref,
    increment_ref,
    asked_ref,
    pulled_ref,
    columns,
    found,
    arrived,
    asked_smem,
    chosen,
    profile,
    slope,
    weight,
    absorb_wide,
    sens_log,
    sens_ln,
    depth,
    transmit,
    sums,
    adjoint,
    wanted,
    upper,
    lower,
    row_of,
    terms,
    sharing,
    field_in,
    kappa_in,
    field,
    east,
    south,
    block_send,
    block_recv,
    edge_send,
    edge_recv,
    local_sems,
):
    dev_count = request_ref.shape[0]
    tile_cols = 64
    me = my_index(lon_count)

    height, breadth, levels = kappa_ref.shape
    tall = height + 2 * HALO
    count = (breadth + 2 * HALO) // SUB
    centre = (pl.ds(HALO, height), pl.ds(HALO, breadth))
    kappa_edges = Edges(
        lat_count, lon_count, kappa_ref, kappa_in, edge_send.at[0], edge_recv.at[0]
    )
    kappa_own = pltpu.make_async_copy(kappa_ref, kappa_in.at[centre], local_sems.at[0])
    kappa_own.start()
    is_first = kappa_edges.lat == 0
    is_last = kappa_edges.lat == lat_count - 1
    for outside, rows in ((is_first, pl.ds(0, HALO)), (is_last, pl.ds(HALO + height, HALO))):

        @pl.when(outside)
        def _(rows=rows):
            kappa_in[rows] = jnp.zeros((HALO,) + kappa_in.shape[1:], F32)
            field_in[rows] = jnp.zeros((HALO,) + field_in.shape[1:], F32)
            field[rows] = jnp.zeros((HALO,) + field.shape[1:], F32)

    slots = dev_count * cap
    feet, channels = observed_ref.shape
    groups = feet // LANES
    parts = channels // SUB
    barrier = greet_all(me, dev_count, lon_count)
    chunk = 256

    @pl.loop(0, background_ref.shape[0] // chunk)
    def _(j):
        at = pl.ds(pl.multiple_of(j * chunk, chunk), chunk)
        columns[at, :] = background_ref[at, :].astype(F32)

    wide = lambda row: jnp.swapaxes(jnp.broadcast_to(row, (LANES, channels)), 0, 1)
    sens = wide(sensitivity_ref[...])
    sens_log[...] = sens * LOG2E
    sens_ln[...] = sens * LN2

    absorb_t = jnp.swapaxes(absorb_ref[...] * (-LOG2E), 0, 1)

    @pl.loop(0, levels // SUB)
    def _(j):
        turned = pltpu.roll(absorb_t, lax.rem(levels - j * SUB, levels), 1)
        for i in range(SUB):
            absorb_wide[j * SUB + i] = jnp.broadcast_to(turned[:, i : i + 1], (channels, LANES))

    pl.semaphore_wait(barrier, dev_count - 1)
    scatter_blocks(
        me, lon_count, request_ref, asked_ref, block_send.at[0], block_recv.at[0]
    )
    kappa_edges.start()

    block = 256 if slots % 256 == 0 else slots

    @pl.loop(0, slots // block)
    def _(j):
        first = pl.multiple_of(j * block, block)
        here = lax.broadcasted_iota(I32, (block, feet), 0) + first == slot_ref[...]
        chosen[pl.ds(first, block), :] = here.astype(F32).astype(BF16)

    for g in range(groups):
        at = pl.ds(g * LANES, LANES)
        accepted = accept_ref[at, :].astype(F32) * variance_ref[...]
        weight[:, at] = jnp.swapaxes(accepted, 0, 1)

    level = lax.broadcasted_iota(I32, (levels, levels * SUB), 0)
    source = lax.broadcasted_iota(I32, (levels, levels * SUB), 1) // SUB
    same = (level == source).astype(F32)
    fall = (level == source + 1).astype(F32) - jnp.where(level == levels - 1, 0.0, same)
    same = same.astype(BF16)
    fall = fall.astype(BF16)

    all_of(asked_ref, block_recv.at[0])
    to_smem = pltpu.make_async_copy(asked_ref, asked_smem, local_sems.at[1])
    to_smem.start()
    to_smem.wait()

    def gather(source):
        for r in range(cap):
            at = asked_smem[source, 0, r]
            total = None
            for k, offset in enumerate((0, 1, tile_cols, tile_cols + 1)):
                share = asked_smem[source, 0, (k + 1) * cap + r].astype(F32)
                term = share * columns[pl.ds(at + offset, 1), :]
                total = term if total is None else total + term
            found[source, r : r + 1, :] = total * (1.0 / FIXED)

    scatter_blocks(
        me, lon_count, found, arrived, block_send.at[1], block_recv.at[1], gather
    )
    all_of(arrived, block_recv.at[1])
    all_of(found, block_send.at[1])

    arrived_t = jnp.swapaxes(arrived[...].reshape(slots, levels), 0, 1)
    high, middle, low = pieces(arrived_t)
    plain = ((1,), (0,))
    mine = dot(high, chosen[...], plain) + dot(middle, chosen[...], plain) + dot(low, chosen[...], plain)
    below = jnp.concatenate([mine[1:, :], mine[levels - 1 :, :]], axis=0)
    for g in range(groups):
        at = slice(g * LANES, (g + 1) * LANES)
        profile[g] = mine[:, at]
        slope[g] = below[:, at] - mine[:, at]

    for g in range(groups):
        at = pl.ds(g * LANES, LANES)

        def descend(l, carry):
            p = profile[g, pl.ds(l, 1), :]
            q = slope[g, pl.ds(l, 1), :]
            out = []
            for c in range(parts):
                rows = slice(c * SUB, (c + 1) * SUB)
                optical, evolved = carry[c]
                layer = absorb_wide[l, rows, :] * jnp.exp2(sens_log[rows, :] * p)
                optical = optical + layer
                passed = jnp.exp2(optical)
                depth[l, rows, :] = layer
                transmit[l, rows, :] = passed
                out.append((optical, evolved + q * passed))
            return tuple(out)

        zero = jnp.zeros((SUB, LANES), F32)
        done = lax.fori_loop(0, levels, descend, ((zero, zero),) * parts, unroll=8)
        top = profile[g, 0:1, :]
        observed_t = jnp.swapaxes(observed_ref[at, :], 0, 1)
        departed = []
        pulls = []
        for c in range(parts):
            rows = slice(c * SUB, (c + 1) * SUB)
            part = observed_t[rows, :] - (done[c][1] + top)
            departed.append(part)
            pulls.append(-(weight[rows, at] * part))
        departure_ref[at, :] = jnp.swapaxes(jnp.concatenate(departed, axis=0), 0, 1)
        whole = pulls[0]
        for c in range(1, parts):
            whole = whole + pulls[c]
        whole = jnp.sum(whole, axis=0, keepdims=True)
        transmit_pull = tuple(pulls)

        def ascend(step, carry):
            l = levels - 1 - step
            q = slope[g, pl.ds(l, 1), :]
            out = []
            passed_sum = None
            layer_sum = None
            for c in range(parts):
                rows = slice(c * SUB, (c + 1) * SUB)
                pulled = transmit_pull[c] * transmit[l, rows, :]
                rest = carry[c] + q * pulled
                through = sens_ln[rows, :] * (depth[l, rows, :] * rest)
                passed_sum = pulled if c == 0 else passed_sum + pulled
                layer_sum = through if c == 0 else layer_sum + through
                out.append(rest)
            at_l = pl.ds(pl.multiple_of(l * SUB, SUB), SUB)
            sums[0, at_l, :] = passed_sum
            sums[1, at_l, :] = layer_sum
            return tuple(out)

        lax.fori_loop(0, levels, ascend, (zero,) * parts, unroll=8)
        total = None
        for matrix, index in ((fall, 0), (same, 1)):
            for piece in pieces(sums[index]):
                term = dot(matrix, piece, plain)
                total = term if total is None else total + term
        first = lax.broadcasted_iota(I32, (levels, LANES), 0) == 0
        adjoint[:, at] = total + jnp.where(first, whole, 0.0)

    parts_adjoint = pieces(adjoint[...])

    @pl.loop(0, slots // block)
    def _(j):
        rows = pl.ds(pl.multiple_of(j * block, block), block)
        total = None
        for piece in parts_adjoint:
            term = dot(chosen[rows, :], piece, ((1,), (1,)))
            total = term if total is None else total + term
        found[pl.ds(pl.multiple_of(j * (block // cap), block // cap), block // cap)] = total.reshape(
            block // cap, cap, levels
        )


    scatter_blocks(me, lon_count, found, pulled_ref, block_send.at[2], block_recv.at[2])

    @pl.loop(0, dev_count)
    def _(source):
        wanted[pl.ds(source, 1), :] = asked_ref[source]

    asked_t = jnp.swapaxes(wanted[...], 0, 1)
    column = lax.broadcasted_iota(I32, (breadth, dev_count), 0)
    shift = breadth.bit_length() - 1
    for r in range(cap):
        base = asked_t[r : r + 1, :]
        base_row = lax.shift_right_logical(base, shift)
        base_col = base - lax.shift_left(base_row, shift)
        shares = [
            asked_t[(k + 1) * cap + r : (k + 1) * cap + r + 1, :].astype(F32) * (1.0 / FIXED)
            for k in range(4)
        ]
        at = slice(r * dev_count, (r + 1) * dev_count)
        row_of[:, at] = base_row.astype(F32)
        for target, first, second in ((upper, shares[0], shares[1]), (lower, shares[2], shares[3])):
            taken = jnp.where(column == base_col, first, 0.0)
            taken = jnp.where(column == base_col + 1, second, taken)
            high = taken.astype(BF16)
            target[0:breadth, at] = high
            target[breadth : 2 * breadth, at] = (taken - high.astype(F32)).astype(BF16)

    kappa_own.wait()
    kappa_edges.sent()
    kappa_edges.arrive()

    def strided(ref, r):
        return tuple(ref[r, pl.ds(i, SUB, stride=count), :] for i in range(count))

    def later(x):
        return pltpu.roll(x, SUB - 1, 0)

    def sooner(x):
        return pltpu.roll(x, 1, 0)

    def conduct(r, here):
        below = strided(kappa_in, jnp.minimum(r + 1, tall - 1))
        for i in range(count):
            beside = here[i + 1] if i + 1 < count else later(here[0])
            east[r, i] = 0.5 * (here[i] + beside)
            south[r, i] = 0.5 * (here[i] + below[i])
        return below

    lax.fori_loop(0, tall, conduct, strided(kappa_in, 0))

    all_of(request_ref, block_send.at[0])
    all_of(found, block_send.at[2])
    all_of(pulled_ref, block_recv.at[2])

    slot_rows = pulled_ref.reshape(slots, levels)
    for r in range(cap):
        pulled = slot_rows[pl.ds(r, dev_count, stride=cap), :]
        high = pulled.astype(BF16)
        at = slice(r * dev_count, (r + 1) * dev_count)
        terms[at, 0:levels] = high
        terms[at, levels : 2 * levels] = (pulled - high.astype(F32)).astype(BF16)

    edges = Edges(
        lat_count,
        lon_count,
        field_in.at[centre],
        field_in,
        edge_send.at[1],
        edge_recv.at[1],
        (height, breadth),
    )
    bands = height // HALO

    @pl.loop(0, bands)
    def _(turn):
        band = jnp.where(turn == 0, 0, jnp.where(turn == 1, bands - 1, turn - 1))
        for g in range(HALO):
            row = (band * HALO + g).astype(F32)
            in_upper = (row_of[...] == row).astype(F32).astype(BF16)
            in_lower = (row_of[...] == row - 1.0).astype(F32).astype(BF16)
            sharing[g * 2 * breadth : (g + 1) * 2 * breadth, :] = (
                upper[...] * in_upper + lower[...] * in_lower
            )
        product = dot(sharing[...], terms[...], ((1,), (0,)))
        for g in range(HALO):
            first = g * 2 * breadth
            second = first + breadth
            raw = (
                product[first:second, 0:levels]
                + product[first:second, levels : 2 * levels]
                + product[second : second + breadth, 0:levels]
            )
            field_in[HALO + band * HALO + g, pl.ds(HALO, breadth), :] = -raw
        for n, (a, b) in enumerate(DIRECTIONS):
            if a == 0:
                edges.copy(n, band).start()

        @pl.when(turn == 1)
        def _():
            edges.start(lambda a: a != 0)

    edges.arrive()
    edges.sent()

    def whole_rows(ref, r):
        return tuple(ref[r, i] for i in range(count))

    for step in range(1, STEPS + 1):
        low = jnp.where(is_first, HALO, jnp.where(is_last, step - step % 2, step))
        high = jnp.where(is_last, HALO + height, tall - step)
        if step == 1:
            load = functools.partial(strided, field_in)
        else:
            load = functools.partial(whole_rows, field)

        def relax_row(r, carry, load=load, step=step):
            here, above = carry
            below = load(jnp.minimum(r + 1, tall - 1))
            down = [south[r, i] * (below[i] - here[i]) for i in range(count)]
            right = []
            for i in range(count):
                beside = here[i + 1] if i + 1 < count else later(here[0])
                right.append(east[r, i] * (beside - here[i]))
            for i in range(count):
                left = right[i - 1] if i > 0 else sooner(right[count - 1])
                new = here[i] + ((right[i] - left) + (down[i] - above[i]))
                if step == STEPS:
                    field_in[r, pl.ds(i, SUB, stride=count), :] = new
                else:
                    field[r, i] = new
            return below, tuple(down)

        def relax(turn, carry, relax_row=relax_row, low=low):
            r = low + 2 * turn
            return relax_row(r + 1, relax_row(r, carry))

        before = load(jnp.maximum(low - 1, 0))
        here = load(low)
        above = tuple(south[jnp.maximum(low - 1, 0), i] * (here[i] - before[i]) for i in range(count))
        lax.fori_loop(0, (high - low + 1) // 2, relax, (here, above))

    result = pltpu.make_async_copy(field_in.at[centre], increment_ref, local_sems.at[0])
    result.start()
    result.wait()


def local(
    lat_count,
    lon_count,
    background,
    diffusivity,
    tile_index,
    anchor,
    weights,
    observed,
    accept,
    absorb,
    sensitivity,
    inverse_variance,
):
    dev_count = lat_count * lon_count
    feet, channels = observed.shape
    cap = max(2, 2 * feet // dev_count)
    height, breadth, levels = background.shape
    slots = dev_count * cap
    width = -(-5 * cap // LANES) * LANES
    shape = jax.ShapeDtypeStruct
    params = functools.partial(pltpu.CompilerParams, vmem_limit_bytes=VMEM_BYTES)
    dma = pltpu.SemaphoreType.DMA

    slot, request = pl.pallas_call(
        functools.partial(request_kernel, cap),
        out_shape=(shape((1, feet), I32), shape((dev_count, 1, width), I32)),
        in_specs=[VMEM_SPEC] * 3,
        out_specs=(VMEM_SPEC, VMEM_SPEC),
        compiler_params=params(),
        name="request",
    )(tile_index.reshape(1, feet), anchor.reshape(1, feet), weights.T)

    wide = (height + 2 * HALO, breadth + 2 * HALO, levels)
    turned = (wide[0], wide[1] // SUB, SUB, levels)
    departure, increment = pl.pallas_call(
        functools.partial(observe_kernel, cap, lat_count, lon_count),
        out_shape=(pltpu.VMEM((feet, channels), F32), pltpu.VMEM((height, breadth, levels), F32)),
        in_specs=[VMEM_SPEC] * 8 + [ANY_SPEC],
        out_specs=(VMEM_SPEC, VMEM_SPEC),
        scratch_shapes=[
            pltpu.VMEM((dev_count, 1, width), I32),
            pltpu.VMEM((dev_count, cap, levels), F32),
            pltpu.VMEM((height * breadth, levels), F32),
            pltpu.VMEM((dev_count, cap, levels), F32),
            pltpu.VMEM((dev_count, cap, levels), F32),
            pltpu.SMEM((dev_count, 1, width), I32),
            pltpu.VMEM((slots, feet), BF16),
            pltpu.VMEM((feet // LANES, levels, LANES), F32),
            pltpu.VMEM((feet // LANES, levels, LANES), F32),
            pltpu.VMEM((channels, feet), F32),
            pltpu.VMEM((levels, channels, LANES), F32),
            pltpu.VMEM((channels, LANES), F32),
            pltpu.VMEM((channels, LANES), F32),
            pltpu.VMEM((levels, channels, LANES), F32),
            pltpu.VMEM((levels, channels, LANES), F32),
            pltpu.VMEM((2, levels * SUB, LANES), F32),
            pltpu.VMEM((levels, feet), F32),
            pltpu.VMEM((dev_count, width), I32),
            pltpu.VMEM((2 * breadth, slots), BF16),
            pltpu.VMEM((2 * breadth, slots), BF16),
            pltpu.VMEM((1, slots), F32),
            pltpu.VMEM((slots, 2 * levels), BF16),
            pltpu.VMEM((HALO * 2 * breadth, slots), BF16),
            pltpu.VMEM(wide, F32),
            pltpu.VMEM(wide, F32),
            pltpu.VMEM(turned, F32),
            pltpu.VMEM(turned, F32),
            pltpu.VMEM(turned, F32),
            dma((3,)),
            dma((3,)),
            dma((2, 8)),
            dma((2, 8)),
            dma((2,)),
        ],
        compiler_params=params(collective_id=0, has_side_effects=True),
        name="observe",
    )(
        slot,
        request,
        background.reshape(height * breadth, levels),
        observed,
        accept,
        absorb,
        sensitivity.reshape(1, channels),
        inverse_variance.reshape(1, channels),
        diffusivity,
    )

    return (departure, increment)


def solution(mesh):
    in_specs = (
        P("lat", "lon", None),
        P("lat", "lon", None),
        P(("lat", "lon"), None),
        P(("lat", "lon")),
        P(("lat", "lon"), None),
        P(("lat", "lon"), None),
        P(("lat", "lon"), None),
        P(),
        P(),
        P(),
    )
    out_specs = (P(("lat", "lon"), None), P("lat", "lon", None))
    return jax.shard_map(
        functools.partial(local, mesh.shape["lat"], mesh.shape["lon"]),
        mesh=mesh,
        in_specs=in_specs,
        out_specs=out_specs,
        check_vma=False,
    )
```

```python
import functools

import jax
import jax.numpy as jnp
from jax import lax
from jax.experimental import pallas as pl
from jax.experimental.pallas import tpu as pltpu
from jax.sharding import PartitionSpec as P

STEPS = 8
HALO = 8
SUB = 8
LANES = 128
LOG2E = 1.4426950408889634
LN2 = 0.6931471805599453
FIXED = 2.0**30
F32 = jnp.float32
BF16 = jnp.bfloat16
I32 = jnp.int32
MESH = pl.DeviceIdType.MESH
VMEM_SPEC = pl.BlockSpec(memory_space=pltpu.VMEM)
SMEM_SPEC = pl.BlockSpec(memory_space=pltpu.SMEM)
ANY_SPEC = pl.BlockSpec(memory_space=pl.ANY)
VMEM_BYTES = 60 * 2**20


def pieces(x):
    high = x.astype(BF16)
    rest = x - high.astype(F32)
    middle = rest.astype(BF16)
    low = (rest - middle.astype(F32)).astype(BF16)
    return high, middle, low


def dot(a, b, contract):
    return lax.dot_general(a, b, (contract, ((), ())), preferred_element_type=F32)


def request_kernel(cap, tile_ref, anchor_ref, weights_ref, slot_ref, request_ref):
    dev_count, _, width = request_ref.shape
    feet = tile_ref.shape[1]
    tile = tile_ref[...]
    named = lax.broadcasted_iota(I32, (dev_count, feet), 0) == tile
    onehot = named.astype(F32).astype(BF16)
    before = (
        lax.broadcasted_iota(I32, (feet, feet), 0) < lax.broadcasted_iota(I32, (feet, feet), 1)
    )
    earlier = dot(onehot, before.astype(F32).astype(BF16), ((1,), (0,)))
    rank = jnp.sum(jnp.where(named, earlier, 0.0), axis=0, keepdims=True).astype(I32)
    slot_ref[...] = tile * cap + rank
    anchor = anchor_ref[...]
    row = ((anchor.astype(F32) + 0.5) * (1.0 / 63.0)).astype(I32)
    base = (anchor + row).astype(F32)
    weights = weights_ref[...]
    shares = weights / jnp.sum(weights, axis=0, keepdims=True)
    place = lax.broadcasted_iota(I32, (cap, feet), 0) == rank
    fields = [base] + [shares[k : k + 1, :] for k in range(4)]
    rows = [jnp.where(place, field, 0.0) for field in fields]
    if width > 5 * cap:
        rows.append(jnp.zeros((width - 5 * cap, feet), F32))
    packed = jnp.concatenate(rows, axis=0)
    high, middle, low = pieces(packed)
    last = ((1,), (1,))
    message = dot(onehot, high, last) + dot(onehot, middle, last) + dot(onehot, low, last)
    scaled = jnp.where(
        lax.broadcasted_iota(I32, (dev_count, width), 1) < cap, message, message * FIXED
    )
    request_ref[...] = scaled.astype(I32).reshape(dev_count, 1, width)


def coordinates(index, lon_count):
    return (index // lon_count, lax.rem(index, lon_count))


def my_index(lon_count):
    return lax.axis_index("lat") * lon_count + lax.axis_index("lon")


def greet_all(me, dev_count, lon_count):
    barrier = pltpu.get_barrier_semaphore()

    @pl.loop(1, dev_count)
    def _(d):
        other = lax.rem(me + d, dev_count)
        pl.semaphore_signal(
            barrier, inc=1, device_id=coordinates(other, lon_count), device_id_type=MESH
        )

    return barrier


def all_of(ref, sem):
    blocks = ref.at[pl.ds(0, ref.shape[0] - 1)]
    pltpu.make_async_copy(blocks, blocks, sem).wait()


def scatter_blocks(me, lon_count, given, taken, send, recv, before=None):
    dev_count = given.shape[0]

    @pl.loop(1, dev_count)
    def _(d):
        other = lax.rem(me + d, dev_count)
        if before is not None:
            before(other)
        pltpu.make_async_remote_copy(
            src_ref=given.at[other],
            dst_ref=taken.at[me],
            send_sem=send,
            recv_sem=recv,
            device_id=coordinates(other, lon_count),
            device_id_type=MESH,
        ).start()

    if before is not None:
        before(me)
    taken[me] = given[me]


DIRECTIONS = [(a, b) for a in (-1, 0, 1) for b in (-1, 0, 1) if (a, b) != (0, 0)]


class Edges:
    def __init__(self, lat_count, lon_count, source, target, send, recv, size=None):
        self.lat_count, self.lon_count = lat_count, lon_count
        self.source, self.target, self.send, self.recv = source, target, send, recv
        self.size = source.shape[:2] if size is None else size
        self.lat, self.lon = lax.axis_index("lat"), lax.axis_index("lon")

    def there(self, a):
        return jnp.logical_and(self.lat + a >= 0, self.lat + a < self.lat_count)

    def device(self, a, b):
        return (self.lat + a, lax.rem(self.lon + b + self.lon_count, self.lon_count))

    def copy(self, n, band=None):
        def span(step, size):
            given = {-1: pl.ds(0, HALO), 0: pl.ds(0, size), 1: pl.ds(size - HALO, HALO)}[step]
            taken = {-1: pl.ds(HALO + size, HALO), 0: pl.ds(HALO, size), 1: pl.ds(0, HALO)}[step]
            return given, taken

        a, b = DIRECTIONS[n]
        given_rows, taken_rows = span(a, self.size[0])
        given_cols, taken_cols = span(b, self.size[1])
        if band is not None:
            given_rows = pl.ds(band * HALO, HALO)
            taken_rows = pl.ds(HALO + band * HALO, HALO)
        return pltpu.make_async_remote_copy(
            src_ref=self.source.at[given_rows, given_cols],
            dst_ref=self.target.at[taken_rows, taken_cols],
            send_sem=self.send.at[n],
            recv_sem=self.recv.at[n],
            device_id=self.device(a, b),
            device_id_type=MESH,
        )

    def each(self, sign, act, which=lambda a: True):
        for n, (a, b) in enumerate(DIRECTIONS):
            if not which(a):
                continue

            @pl.when(self.there(sign * a))
            def _(n=n):
                act(self.copy(n))

    def start(self, which=lambda a: True):
        self.each(1, lambda copy: copy.start(), which)

    def arrive(self):
        self.each(-1, lambda copy: copy.wait_recv())

    def sent(self):
        self.each(1, lambda copy: copy.wait_send())


def observe_kernel(
    cap,
    lat_count,
    lon_count,
    slot_ref,
    request_ref,
    background_ref,
    observed_ref,
    accept_ref,
    absorb_ref,
    sensitivity_ref,
    variance_ref,
    kappa_ref,
    departure_ref,
    increment_ref,
    asked_ref,
    pulled_ref,
    columns,
    found,
    arrived,
    asked_smem,
    chosen,
    profile,
    slope,
    weight,
    absorb_wide,
    sens_log,
    sens_ln,
    depth,
    transmit,
    sums,
    adjoint,
    wanted,
    upper,
    lower,
    row_of,
    terms,
    sharing,
    field_in,
    kappa_in,
    field,
    east,
    south,
    block_send,
    block_recv,
    edge_send,
    edge_recv,
    local_sems,
):
    dev_count = request_ref.shape[0]
    tile_cols = 64
    me = my_index(lon_count)

    height, breadth, levels = kappa_ref.shape
    tall = height + 2 * HALO
    count = (breadth + 2 * HALO) // SUB
    centre = (pl.ds(HALO, height), pl.ds(HALO, breadth))
    kappa_edges = Edges(
        lat_count, lon_count, kappa_ref, kappa_in, edge_send.at[0], edge_recv.at[0]
    )
    kappa_own = pltpu.make_async_copy(kappa_ref, kappa_in.at[centre], local_sems.at[0])
    kappa_own.start()
    is_first = kappa_edges.lat == 0
    is_last = kappa_edges.lat == lat_count - 1
    for outside, rows in ((is_first, pl.ds(0, HALO)), (is_last, pl.ds(HALO + height, HALO))):

        @pl.when(outside)
        def _(rows=rows):
            kappa_in[rows] = jnp.zeros((HALO,) + kappa_in.shape[1:], F32)
            field_in[rows] = jnp.zeros((HALO,) + field_in.shape[1:], F32)
            field[rows] = jnp.zeros((HALO,) + field.shape[1:], F32)

    slots = dev_count * cap
    feet, channels = observed_ref.shape
    groups = feet // LANES
    parts = channels // SUB
    barrier = greet_all(me, dev_count, lon_count)
    chunk = 256

    @pl.loop(0, background_ref.shape[0] // chunk)
    def _(j):
        at = pl.ds(pl.multiple_of(j * chunk, chunk), chunk)
        columns[at, :] = background_ref[at, :].astype(F32)

    wide = lambda row: jnp.swapaxes(jnp.broadcast_to(row, (LANES, channels)), 0, 1)
    sens = wide(sensitivity_ref[...])
    sens_log[...] = sens * LOG2E
    sens_ln[...] = sens * LN2

    absorb_t = jnp.swapaxes(absorb_ref[...] * (-LOG2E), 0, 1)

    @pl.loop(0, levels // SUB)
    def _(j):
        turned = pltpu.roll(absorb_t, lax.rem(levels - j * SUB, levels), 1)
        for i in range(SUB):
            absorb_wide[j * SUB + i] = jnp.broadcast_to(turned[:, i : i + 1], (channels, LANES))

    pl.semaphore_wait(barrier, dev_count - 1)
    scatter_blocks(
        me, lon_count, request_ref, asked_ref, block_send.at[0], block_recv.at[0]
    )
    kappa_edges.start()

    block = 256 if slots % 256 == 0 else slots

    @pl.loop(0, slots // block)
    def _(j):
        first = pl.multiple_of(j * block, block)
        here = lax.broadcasted_iota(I32, (block, feet), 0) + first == slot_ref[...]
        chosen[pl.ds(first, block), :] = here.astype(F32).astype(BF16)

    for g in range(groups):
        at = pl.ds(g * LANES, LANES)
        accepted = accept_ref[at, :].astype(F32) * variance_ref[...]
        weight[:, at] = jnp.swapaxes(accepted, 0, 1)

    level = lax.broadcasted_iota(I32, (levels, levels * SUB), 0)
    source = lax.broadcasted_iota(I32, (levels, levels * SUB), 1) // SUB
    same = (level == source).astype(F32)
    fall = (level == source + 1).astype(F32) - jnp.where(level == levels - 1, 0.0, same)
    same = same.astype(BF16)
    fall = fall.astype(BF16)

    all_of(asked_ref, block_recv.at[0])
    to_smem = pltpu.make_async_copy(asked_ref, asked_smem, local_sems.at[1])
    to_smem.start()
    to_smem.wait()

    def gather(source):
        for r in range(cap):
            at = asked_smem[source, 0, r]
            total = None
            for k, offset in enumerate((0, 1, tile_cols, tile_cols + 1)):
                share = asked_smem[source, 0, (k + 1) * cap + r].astype(F32)
                term = share * columns[pl.ds(at + offset, 1), :]
                total = term if total is None else total + term
            found[source, r : r + 1, :] = total * (1.0 / FIXED)

    scatter_blocks(
        me, lon_count, found, arrived, block_send.at[1], block_recv.at[1], gather
    )
    all_of(arrived, block_recv.at[1])
    all_of(found, block_send.at[1])

    arrived_t = jnp.swapaxes(arrived[...].reshape(slots, levels), 0, 1)
    high, middle, _ = pieces(arrived_t)
    plain = ((1,), (0,))
    mine = dot(high, chosen[...], plain) + dot(middle, chosen[...], plain)
    below = jnp.concatenate([mine[1:, :], mine[levels - 1 :, :]], axis=0)
    for g in range(groups):
        at = slice(g * LANES, (g + 1) * LANES)
        profile[g] = mine[:, at]
        slope[g] = below[:, at] - mine[:, at]

    for g in range(groups):
        at = pl.ds(g * LANES, LANES)

        def descend(l, carry):
            p = profile[g, pl.ds(l, 1), :]
            q = slope[g, pl.ds(l, 1), :]
            out = []
            for c in range(parts):
                rows = slice(c * SUB, (c + 1) * SUB)
                optical, evolved = carry[c]
                layer = absorb_wide[l, rows, :] * jnp.exp2(sens_log[rows, :] * p)
                optical = optical + layer
                passed = jnp.exp2(optical)
                depth[l, rows, :] = layer
                transmit[l, rows, :] = passed
                out.append((optical, evolved + q * passed))
            return tuple(out)

        zero = jnp.zeros((SUB, LANES), F32)
        done = lax.fori_loop(0, levels, descend, ((zero, zero),) * parts, unroll=16)
        top = profile[g, 0:1, :]
        observed_t = jnp.swapaxes(observed_ref[at, :], 0, 1)
        departed = []
        pulls = []
        for c in range(parts):
            rows = slice(c * SUB, (c + 1) * SUB)
            part = observed_t[rows, :] - (done[c][1] + top)
            departed.append(part)
            pulls.append(-(weight[rows, at] * part))
        departure_ref[at, :] = jnp.swapaxes(jnp.concatenate(departed, axis=0), 0, 1)
        whole = pulls[0]
        for c in range(1, parts):
            whole = whole + pulls[c]
        whole = jnp.sum(whole, axis=0, keepdims=True)
        transmit_pull = tuple(pulls)

        def ascend(step, carry):
            l = levels - 1 - step
            q = slope[g, pl.ds(l, 1), :]
            out = []
            passed_sum = None
            layer_sum = None
            for c in range(parts):
                rows = slice(c * SUB, (c + 1) * SUB)
                pulled = transmit_pull[c] * transmit[l, rows, :]
                rest = carry[c] + q * pulled
                through = sens_ln[rows, :] * (depth[l, rows, :] * rest)
                passed_sum = pulled if c == 0 else passed_sum + pulled
                layer_sum = through if c == 0 else layer_sum + through
                out.append(rest)
            at_l = pl.ds(pl.multiple_of(l * SUB, SUB), SUB)
            sums[0, at_l, :] = passed_sum
            sums[1, at_l, :] = layer_sum
            return tuple(out)

        lax.fori_loop(0, levels, ascend, (zero,) * parts, unroll=16)
        total = None
        for matrix, index in ((fall, 0), (same, 1)):
            for piece in pieces(sums[index]):
                term = dot(matrix, piece, plain)
                total = term if total is None else total + term
        first = lax.broadcasted_iota(I32, (levels, LANES), 0) == 0
        adjoint[:, at] = total + jnp.where(first, whole, 0.0)

    parts_adjoint = pieces(adjoint[...])[:2]

    @pl.loop(0, slots // block)
    def _(j):
        rows = pl.ds(pl.multiple_of(j * block, block), block)
        total = None
        for piece in parts_adjoint:
            term = dot(chosen[rows, :], piece, ((1,), (1,)))
            total = term if total is None else total + term
        found[pl.ds(pl.multiple_of(j * (block // cap), block // cap), block // cap)] = total.reshape(
            block // cap, cap, levels
        )


    scatter_blocks(me, lon_count, found, pulled_ref, block_send.at[2], block_recv.at[2])

    @pl.loop(0, dev_count)
    def _(source):
        wanted[pl.ds(source, 1), :] = asked_ref[source]

    asked_t = jnp.swapaxes(wanted[...], 0, 1)
    column = lax.broadcasted_iota(I32, (breadth, dev_count), 0)
    shift = breadth.bit_length() - 1
    for r in range(cap):
        base = asked_t[r : r + 1, :]
        base_row = lax.shift_right_logical(base, shift)
        base_col = base - lax.shift_left(base_row, shift)
        shares = [
            asked_t[(k + 1) * cap + r : (k + 1) * cap + r + 1, :].astype(F32) * (1.0 / FIXED)
            for k in range(4)
        ]
        at = slice(r * dev_count, (r + 1) * dev_count)
        row_of[:, at] = base_row.astype(F32)
        for target, first, second in ((upper, shares[0], shares[1]), (lower, shares[2], shares[3])):
            taken = jnp.where(column == base_col, first, 0.0)
            taken = jnp.where(column == base_col + 1, second, taken)
            high = taken.astype(BF16)
            target[0:breadth, at] = high
            target[breadth : 2 * breadth, at] = (taken - high.astype(F32)).astype(BF16)

    kappa_own.wait()
    kappa_edges.sent()
    kappa_edges.arrive()

    def strided(ref, r):
        return tuple(ref[r, pl.ds(i, SUB, stride=count), :] for i in range(count))

    def later(x):
        return pltpu.roll(x, SUB - 1, 0)

    def sooner(x):
        return pltpu.roll(x, 1, 0)

    def conduct(r, here):
        below = strided(kappa_in, jnp.minimum(r + 1, tall - 1))
        for i in range(count):
            beside = here[i + 1] if i + 1 < count else later(here[0])
            east[r, i] = 0.5 * (here[i] + beside)
            south[r, i] = 0.5 * (here[i] + below[i])
        return below

    lax.fori_loop(0, tall, conduct, strided(kappa_in, 0))

    all_of(request_ref, block_send.at[0])
    all_of(found, block_send.at[2])
    all_of(pulled_ref, block_recv.at[2])

    slot_rows = pulled_ref.reshape(slots, levels)
    for r in range(cap):
        pulled = slot_rows[pl.ds(r, dev_count, stride=cap), :]
        high = pulled.astype(BF16)
        at = slice(r * dev_count, (r + 1) * dev_count)
        terms[at, 0:levels] = high
        terms[at, levels : 2 * levels] = (pulled - high.astype(F32)).astype(BF16)

    edges = Edges(
        lat_count,
        lon_count,
        field_in.at[centre],
        field_in,
        edge_send.at[1],
        edge_recv.at[1],
        (height, breadth),
    )
    bands = height // HALO

    @pl.loop(0, bands)
    def _(turn):
        band = jnp.where(turn == 0, 0, jnp.where(turn == 1, bands - 1, turn - 1))
        for g in range(HALO):
            row = (band * HALO + g).astype(F32)
            in_upper = (row_of[...] == row).astype(F32).astype(BF16)
            in_lower = (row_of[...] == row - 1.0).astype(F32).astype(BF16)
            sharing[g * 2 * breadth : (g + 1) * 2 * breadth, :] = (
                upper[...] * in_upper + lower[...] * in_lower
            )
        product = dot(sharing[...], terms[...], ((1,), (0,)))
        for g in range(HALO):
            first = g * 2 * breadth
            second = first + breadth
            raw = (
                product[first:second, 0:levels]
                + product[first:second, levels : 2 * levels]
                + product[second : second + breadth, 0:levels]
            )
            field_in[HALO + band * HALO + g, pl.ds(HALO, breadth), :] = -raw
        for n, (a, b) in enumerate(DIRECTIONS):
            if a == 0:
                edges.copy(n, band).start()

        @pl.when(turn == 1)
        def _():
            edges.start(lambda a: a != 0)

    edges.arrive()
    edges.sent()

    def whole_rows(ref, r):
        return tuple(ref[r, i] for i in range(count))

    for step in range(1, STEPS + 1):
        low = jnp.where(is_first, HALO, jnp.where(is_last, step - step % 2, step))
        high = jnp.where(is_last, HALO + height, tall - step)
        if step == 1:
            load = functools.partial(strided, field_in)
        else:
            load = functools.partial(whole_rows, field)

        def relax_row(r, carry, load=load, step=step):
            here, above = carry
            below = load(jnp.minimum(r + 1, tall - 1))
            down = [south[r, i] * (below[i] - here[i]) for i in range(count)]
            right = []
            for i in range(count):
                beside = here[i + 1] if i + 1 < count else later(here[0])
                right.append(east[r, i] * (beside - here[i]))
            for i in range(count):
                left = right[i - 1] if i > 0 else sooner(right[count - 1])
                new = here[i] + ((right[i] - left) + (down[i] - above[i]))
                if step == STEPS:
                    field_in[r, pl.ds(i, SUB, stride=count), :] = new
                else:
                    field[r, i] = new
            return below, tuple(down)

        def relax(turn, carry, relax_row=relax_row, low=low):
            r = low + 2 * turn
            return relax_row(r + 1, relax_row(r, carry))

        before = load(jnp.maximum(low - 1, 0))
        here = load(low)
        above = tuple(south[jnp.maximum(low - 1, 0), i] * (here[i] - before[i]) for i in range(count))
        lax.fori_loop(0, (high - low + 1) // 2, relax, (here, above))

    result = pltpu.make_async_copy(field_in.at[centre], increment_ref, local_sems.at[0])
    result.start()
    result.wait()


def local(
    lat_count,
    lon_count,
    background,
    diffusivity,
    tile_index,
    anchor,
    weights,
    observed,
    accept,
    absorb,
    sensitivity,
    inverse_variance,
):
    dev_count = lat_count * lon_count
    feet, channels = observed.shape
    cap = max(2, 2 * feet // dev_count)
    height, breadth, levels = background.shape
    slots = dev_count * cap
    width = -(-5 * cap // LANES) * LANES
    shape = jax.ShapeDtypeStruct
    params = functools.partial(pltpu.CompilerParams, vmem_limit_bytes=VMEM_BYTES)
    dma = pltpu.SemaphoreType.DMA

    slot, request = pl.pallas_call(
        functools.partial(request_kernel, cap),
        out_shape=(shape((1, feet), I32), shape((dev_count, 1, width), I32)),
        in_specs=[VMEM_SPEC] * 3,
        out_specs=(VMEM_SPEC, VMEM_SPEC),
        compiler_params=params(),
        name="request",
    )(tile_index.reshape(1, feet), anchor.reshape(1, feet), weights.T)

    wide = (height + 2 * HALO, breadth + 2 * HALO, levels)
    turned = (wide[0], wide[1] // SUB, SUB, levels)
    departure, increment = pl.pallas_call(
        functools.partial(observe_kernel, cap, lat_count, lon_count),
        out_shape=(pltpu.VMEM((feet, channels), F32), pltpu.VMEM((height, breadth, levels), F32)),
        in_specs=[VMEM_SPEC] * 8 + [ANY_SPEC],
        out_specs=(VMEM_SPEC, VMEM_SPEC),
        scratch_shapes=[
            pltpu.VMEM((dev_count, 1, width), I32),
            pltpu.VMEM((dev_count, cap, levels), F32),
            pltpu.VMEM((height * breadth, levels), F32),
            pltpu.VMEM((dev_count, cap, levels), F32),
            pltpu.VMEM((dev_count, cap, levels), F32),
            pltpu.SMEM((dev_count, 1, width), I32),
            pltpu.VMEM((slots, feet), BF16),
            pltpu.VMEM((feet // LANES, levels, LANES), F32),
            pltpu.VMEM((feet // LANES, levels, LANES), F32),
            pltpu.VMEM((channels, feet), F32),
            pltpu.VMEM((levels, channels, LANES), F32),
            pltpu.VMEM((channels, LANES), F32),
            pltpu.VMEM((channels, LANES), F32),
            pltpu.VMEM((levels, channels, LANES), F32),
            pltpu.VMEM((levels, channels, LANES), F32),
            pltpu.VMEM((2, levels * SUB, LANES), F32),
            pltpu.VMEM((levels, feet), F32),
            pltpu.VMEM((dev_count, width), I32),
            pltpu.VMEM((2 * breadth, slots), BF16),
            pltpu.VMEM((2 * breadth, slots), BF16),
            pltpu.VMEM((1, slots), F32),
            pltpu.VMEM((slots, 2 * levels), BF16),
            pltpu.VMEM((HALO * 2 * breadth, slots), BF16),
            pltpu.VMEM(wide, F32),
            pltpu.VMEM(wide, F32),
            pltpu.VMEM(turned, F32),
            pltpu.VMEM(turned, F32),
            pltpu.VMEM(turned, F32),
            dma((3,)),
            dma((3,)),
            dma((2, 8)),
            dma((2, 8)),
            dma((2,)),
        ],
        compiler_params=params(collective_id=0, has_side_effects=True),
        name="observe",
    )(
        slot,
        request,
        background.reshape(height * breadth, levels),
        observed,
        accept,
        absorb,
        sensitivity.reshape(1, channels),
        inverse_variance.reshape(1, channels),
        diffusivity,
    )

    return (departure, increment)


def solution(mesh):
    in_specs = (
        P("lat", "lon", None),
        P("lat", "lon", None),
        P(("lat", "lon"), None),
        P(("lat", "lon")),
        P(("lat", "lon"), None),
        P(("lat", "lon"), None),
        P(("lat", "lon"), None),
        P(),
        P(),
        P(),
    )
    out_specs = (P(("lat", "lon"), None), P("lat", "lon", None))
    return jax.shard_map(
        functools.partial(local, mesh.shape["lat"], mesh.shape["lon"]),
        mesh=mesh,
        in_specs=in_specs,
        out_specs=out_specs,
        check_vma=False,
    )
```
